128 devices in a mesh: tm: 8 (over x, z_lo), space: 16 (over y, z_hi, core).
Axes of the slice: x: 4, y: 4, z: 4 (z_hi: 2, z_lo: 2; z = z_hi * 2 + z_lo), core: 2. Of those that a mesh axis runs over, the one named last changes fastest.
Arguments:
- flow_state: float32 [16, 4, 64, 64, 128], P('tm', None, 'space'), may hold values from -6 to 6
- adjoint_state: float32 [16, 4, 64, 64, 128], P('tm', None, 'space'), may hold values from -6 to 6
- density: float32 [64, 64, 128], P('space'), may hold values from 0 to 1
- design_mask: int32 [64, 64, 128], P('space'), may hold values 0 or 1
- labels: int32 [64, 64, 128], P('space'), may hold values from 0 to 2
Outputs:
- flow_residual: float32 [16, 4, 64, 64, 128], P('tm', None, 'space')
- adjoint_residual: float32 [16, 4, 64, 64, 128], P('tm', None, 'space')
The draws below stay inside these ranges and needn't reach their ends.
All inputs are finite; a program needn't handle non-finite values. No bound on the sum of `design_mask` on one device may be relied on, other than what follows from the above.
Results may differ from the reference program's by a relative error of at most 0.0001.
Values sent between devices are 32-bit elements; how exact they have to be, the bound alone decides.
No kernel may reach another device: no remote copies, remote signals or barrier semaphores. Data moves between devices by JAX's collectives and lax.ppermute only.
A program may use at most 256 MiB of HBM per device.

```python
import jax
import jax.numpy as jnp
from jax import lax

NT = 16
NY = 64
NZ = 128
NX = 64


def place_ends(result, rng, smallest, largest):
    longest = result.shape.index(max(result.shape))
    spots = []
    for shift in (0, 1):
        where = [jax.random.randint(jax.random.fold_in(rng, axis), (), 0, length) for axis, length in enumerate(result.shape)]
        where[longest] = (where[longest] + shift) % result.shape[longest]
        spots.append(tuple(where))
    return result.at[spots[0]].set(smallest).at[spots[1]].set(largest)


def steps_of(own_key, dims, cuts, smallest, top_value):
    gain = 1.0
    for dim, shards_of in cuts:
        draws = jax.random.uniform(jax.random.fold_in(jax.random.fold_in(own_key, 6), dim), (shards_of,), jnp.float32, smallest / len(cuts), top_value / len(cuts))
        gain = gain * jnp.repeat(jnp.exp(draws), dims[dim] // shards_of).reshape((-1,) + (1,) * (len(dims) - 1 - dim))
    return gain


def normal_values(key, dims, scale, most, split=(), kind=jnp.bfloat16):
    entries = jax.random.normal(key, dims, jnp.float32) * scale
    if len(split) > 0:
        entries = steps_of(key, dims, split, -0.22, 0.18) * entries
    return jnp.clip(entries, min=-most, max=most).astype(kind)


def setup_inputs(seed: int = 0) -> dict:
    seeds = jax.random.split(jax.random.key(seed), 6)
    flow_state = normal_values(seeds[0], (NT, 4, NX, NY, NZ), 1.0, 6.0, ((0, 8), (2, 16)), jnp.float32)
    adjoint_state = normal_values(seeds[1], (NT, 4, NX, NY, NZ), 1.0, 6.0, ((0, 8), (2, 16)), jnp.float32)
    density = jnp.clip(1.0 * jax.random.uniform(seeds[2], (NX, NY, NZ), jnp.float32) ** steps_of(seeds[2], (NX, NY, NZ), ((0, 16),), -0.2, 0.2), 0.0, 1.0)
    design_mask = place_ends((jax.random.randint(seeds[3], (NX, NY, NZ), 0, 2) < 1).astype(jnp.int32), jax.random.fold_in(seeds[3], 1), 0, 1)
    labels = place_ends(jax.random.randint(seeds[4], (NX, NY, NZ), 0, 3), jax.random.fold_in(seeds[4], 1), 0, 2).astype(jnp.int32)
    return dict(flow_state=flow_state, adjoint_state=adjoint_state, density=density, design_mask=design_mask, labels=labels)


NU_INF = 0.0616
NU_ZERO = 1.0
LAMBDA_SQ = 3.313 * 3.313
POWER = (0.3568 - 1.0) / 2.0
BRINKMAN_MAX = 8.0
RAMP_SHAPE = 0.1
TIME_SCALE = 0.25

def spectral_matrix(points):
    index = jnp.arange(points, dtype=jnp.int32)
    offset = index[:, None] - index[None, :]
    parity = (1 - 2 * (offset % 2)).astype(jnp.float32)
    angle = jnp.pi * offset.astype(jnp.float32) / points
    angle = jnp.where(offset == 0, 0.5 * jnp.pi, angle)
    table = TIME_SCALE * 0.5 * parity * jnp.cos(angle) / jnp.sin(angle)
    return jnp.where(offset == 0, 0.0, table)

def central(source, direction):
    along = source.ndim - 3 + direction
    extent = source.shape[along]
    upper_part = lax.slice_in_dim(source, 2, extent, axis=along)
    lower_part = lax.slice_in_dim(source, 0, extent - 2, axis=along)
    return 0.5 * (upper_part - lower_part)

def trim_edges(source, directions):
    for direction in directions:
        along = source.ndim - 3 + direction
        source = lax.slice_in_dim(source, 1, source.shape[along] - 1, axis=along)
    return source

def derivative(source, direction):
    others = [k for k in range(3) if k != direction]
    return trim_edges(central(source, direction), others)

def spatial(padded):
    widened = jnp.pad(padded, ((0, 0), (0, 0), (2, 2), (2, 2)))
    velocity = widened[:3]
    pressure = widened[3]
    gradients = [derivative(velocity, k) for k in range(3)]
    strain = [[0.5 * (gradients[k][j] + gradients[j][k]) for k in range(3)] for j in range(3)]
    shear_sq = 2.0 * sum((strain[j][k] * strain[j][k] for j in range(3) for k in range(3)))
    viscosity = NU_INF + (NU_ZERO - NU_INF) * jnp.power(1.0 + LAMBDA_SQ * shear_sq, POWER)
    center_vel = velocity[:, 2:-2, 2:-2, 2:-2]
    momentum = []
    for j in range(3):
        convection = sum((center_vel[k] * trim_edges(gradients[k][j], (0, 1, 2)) for k in range(3)))
        diffusion = sum((derivative(2.0 * viscosity * strain[j][k], k) for k in range(3)))
        press_grad = trim_edges(derivative(pressure, j), (0, 1, 2))
        momentum.append(convection - diffusion + press_grad)
    divergence = sum((trim_edges(gradients[k][k], (0, 1, 2)) for k in range(3)))
    return jnp.stack(momentum + [divergence])

def brinkman(density, design_mask, labels):
    design = jnp.where(design_mask == 1, density, 1.0)
    ramp = BRINKMAN_MAX * RAMP_SHAPE * (1.0 - design) / (RAMP_SHAPE + design)
    penalty = jnp.where(labels == 0, ramp, BRINKMAN_MAX)
    return (penalty, labels == 2)

def assemble(state_now, adjoint_now, spatial_res, pulled, time_forward, time_adjoint, penalty, inlet_cells, instance):
    inflow = 1.0 + 0.5 * jnp.sin(2.0 * jnp.pi * instance.astype(jnp.float32) / NT)
    forcing = penalty * state_now[:3]
    forcing = forcing.at[0].add(-jnp.where(inlet_cells, penalty * inflow, 0.0))
    flow_part = jnp.concatenate([spatial_res[:3] + time_forward + forcing, spatial_res[3:]], axis=0)
    adjoint_part = jnp.concatenate([pulled[:3] + time_adjoint + penalty * adjoint_now[:3], pulled[3:]], axis=0)
    return (flow_part, adjoint_part)

def reference(flow_state, adjoint_state, density, design_mask, labels):
    spectral = spectral_matrix(NT)
    time_forward = jnp.einsum('nm,mcxyz->ncxyz', spectral, flow_state[:, :3], precision=lax.Precision.HIGHEST)
    time_adjoint = jnp.einsum('mn,mcxyz->ncxyz', spectral, adjoint_state[:, :3], precision=lax.Precision.HIGHEST)
    penalty, inlet_cells = brinkman(density, design_mask, labels)

    def per_instance(members):
        state_now, adjoint_now, forward_now, backward_now, instance = members
        padded = jnp.pad(state_now, ((0, 0), (2, 2), (0, 0), (0, 0)))
        spatial_res, pullback = jax.vjp(spatial, padded)
        pulled, = pullback(adjoint_now)
        pulled = pulled[:, 2:-2]
        return assemble(state_now, adjoint_now, spatial_res, pulled, forward_now, backward_now, penalty, inlet_cells, instance)
    flow_residual, adjoint_residual = lax.map(per_instance, (flow_state, adjoint_state, time_forward, time_adjoint, jnp.arange(NT, dtype=jnp.int32)))
    return (flow_residual, adjoint_residual)
```

```python
import jax
import jax.numpy as jnp
from jax import lax
from jax.experimental import pallas as pl
from jax.experimental.pallas import tpu as pltpu
from jax.sharding import PartitionSpec as P
import numpy as np

NT = 16
NU_INF = 0.0616
NU_ZERO = 1.0
LAMBDA_SQ = 3.313 * 3.313
POWER = (0.3568 - 1.0) / 2.0
BRINKMAN_MAX = 8.0
RAMP_SHAPE = 0.1
TIME_SCALE = 0.25

PLANES = 4
ROWS = 64
LANES = 128
TOP = 8
PADDED = ROWS + 2 * TOP

MU_A = 0.25 * NU_INF
MU_B = 0.25 * (NU_ZERO - NU_INF)
SHEAR = LAMBDA_SQ / 8.0
DMU = (NU_ZERO - NU_INF) * POWER * LAMBDA_SQ / 16.0


def viscosity(square_sum):
    q = 1.0 + SHEAR * square_sum
    log_q = jnp.log(q)
    return MU_A + MU_B * jnp.exp(POWER * log_q), DMU * jnp.exp((POWER - 1.0) * log_q)


def outer_cell(u, lam, axis):
    strain = [u[j] + u[j] if j == axis else u[j] for j in range(3)]
    rate = [lam[j] + lam[j] if j == axis else lam[j] for j in range(3)]
    others = [j for j in range(3) if j != axis]
    square = sum(strain[j] * strain[j] for j in others)
    cross = sum(strain[j] * rate[j] for j in others)
    square = square + square + strain[axis] * strain[axis]
    cross = cross + cross + strain[axis] * rate[axis]
    mu, dmu = viscosity(square)
    slope = dmu * cross
    return [mu * s for s in strain], [mu * e + slope * s for s, e in zip(strain, rate)]


def stencil_kernel(
    inflow_ref, flow_ref, adj_ref, low_ref, high_ref, density_ref, mask_ref, labels_ref,
    out_f, out_a, w, tx, fx, ty, fy, sems,
):
    insts = out_f.shape[0]
    rows = pl.ds(TOP, ROWS)
    copies = []
    for source, base, last in ((flow_ref, 0, 6), (adj_ref, 3, 7)):
        copies.append((source.at[:, 0:3], w.at[:, base : base + 3, 2:6, rows, :]))
        copies.append((source.at[:, 3], w.at[:, last, 2:6, rows, :]))
    for source, first in ((low_ref, 0), (high_ref, 6)):
        for c in range(6):
            copies.append((source.at[:, 2 * c : 2 * c + 2], w.at[:, c, first : first + 2, rows, :]))
        near = 1 if first == 0 else 6
        copies.append((source.at[:, 12:14], w.at[:, 6:8, near, rows, :]))
    handles = [pltpu.make_async_copy(a, b, sems.at[i]) for i, (a, b) in enumerate(copies)]
    for h in handles:
        h.start()
    zero = jnp.zeros((TOP, LANES), jnp.float32)

    def clear(i, _):
        for c in range(6):
            for p in range(8):
                w[i, c, p, 0:TOP, :] = zero
                w[i, c, p, TOP + ROWS : PADDED, :] = zero
        return 0

    lax.fori_loop(0, insts, clear, 0)
    for h in handles:
        h.wait()

    lane = lax.broadcasted_iota(jnp.int32, (8, LANES), 1)
    is_first = lane == 0
    is_last = lane == LANES - 1

    def along_z(f):
        up = jnp.where(is_last, 0.0, pltpu.roll(f, LANES - 1, 1))
        down = jnp.where(is_first, 0.0, pltpu.roll(f, 1, 1))
        return up - down

    def along_z_outer(f, outer):
        up = jnp.where(is_last, -outer, pltpu.roll(f, LANES - 1, 1))
        down = jnp.where(is_first, outer, pltpu.roll(f, 1, 1))
        return up - down

    def tile_work(i, p, t, interior):
        r = TOP + pl.multiple_of(t * 8, 8)
        here = pl.ds(r, 8)
        u = [w[i, j, p, here, :] for j in range(3)]
        lam = [w[i, 3 + j, p, here, :] for j in range(3)]
        grads, rates = [], []
        for base, values, into in ((0, u, grads), (3, lam, rates)):
            into.append([w[i, base + j, p + 1, here, :] - w[i, base + j, p - 1, here, :] for j in range(3)])
            into.append(
                [w[i, base + j, p, pl.ds(r + 1, 8), :] - w[i, base + j, p, pl.ds(r - 1, 8), :] for j in range(3)]
            )
            into.append([along_z(v) for v in values])
        strain = [[grads[k][j] + grads[j][k] for k in range(3)] for j in range(3)]
        rate = [[rates[k][j] + rates[j][k] for k in range(3)] for j in range(3)]
        pairs = ((0, 1), (0, 2), (1, 2))
        square = sum(strain[j][k] * strain[j][k] for j, k in pairs)
        cross = sum(strain[j][k] * rate[j][k] for j, k in pairs)
        square = square + square + sum(strain[j][j] * strain[j][j] for j in range(3))
        cross = cross + cross + sum(strain[j][j] * rate[j][j] for j in range(3))
        mu, dmu = viscosity(square)
        slope = dmu * cross
        half_u = [0.5 * v for v in u]
        half_p = 0.5 * w[i, 6, p, here, :]
        half_q = 0.5 * w[i, 7, p, here, :]

        def flux(j, k):
            t_jk = mu * strain[j][k]
            f_jk = mu * rate[j][k] + slope * strain[j][k] + half_u[k] * lam[j]
            if j == k:
                t_jk, f_jk = t_jk - half_p, f_jk + half_q
            return t_jk, f_jk

        for j in range(3):
            t_jk, f_jk = flux(j, 0)
            tx[j, p, pl.ds(r - TOP, 8), :] = t_jk
            fx[j, p, pl.ds(r - TOP, 8), :] = f_jk
        if not interior:
            return
        q = p - 2
        out_rows = pl.ds(r - TOP, 8)
        for j in range(3):
            t_jk, f_jk = flux(j, 1)
            ty[j, q, here, :] = t_jk
            fy[j, q, here, :] = f_jk
        outer_t, outer_f = outer_cell(u, lam, 2)
        design = jnp.where(mask_ref[q, out_rows, :] == 1, density_ref[q, out_rows, :], 1.0)
        label = labels_ref[q, out_rows, :]
        ramp = (BRINKMAN_MAX * RAMP_SHAPE) * (1.0 - design) / (RAMP_SHAPE + design)
        penalty = jnp.where(label == 0, ramp, BRINKMAN_MAX)
        target = jnp.where(label == 2, inflow_ref[i], 0.0)
        half_lam = [0.5 * v for v in lam]
        for j in range(3):
            t_jk, f_jk = flux(j, 2)
            shifted = u[j] - target if j == 0 else u[j]
            out_f[i, j, q, out_rows, :] = (
                sum(half_u[k] * grads[k][j] for k in range(3)) - along_z_outer(t_jk, outer_t[j]) + penalty * shifted
            )
            out_a[i, j, q, out_rows, :] = (
                sum(half_lam[k] * grads[j][k] for k in range(3)) - along_z_outer(f_jk, outer_f[j]) + penalty * lam[j]
            )
        out_f[i, 3, q, out_rows, :] = 0.25 * (strain[0][0] + strain[1][1] + strain[2][2])
        out_a[i, 3, q, out_rows, :] = -0.25 * (rate[0][0] + rate[1][1] + rate[2][2])

    def y_edges(i, q):
        p = q + 2
        for first, keep, row, sign in ((TOP, 0, TOP - 1, 1.0), (TOP + ROWS - 8, 7, TOP + ROWS, -1.0)):
            u = [w[i, j, p, first : first + 8, :] for j in range(3)]
            lam = [w[i, 3 + j, p, first : first + 8, :] for j in range(3)]
            outer_t, outer_f = outer_cell(u, lam, 1)
            for j in range(3):
                ty[j, q, row : row + 1, :] = sign * outer_t[j][keep : keep + 1]
                fy[j, q, row : row + 1, :] = sign * outer_f[j][keep : keep + 1]

    def instance(i, _):
        def outer_planes(n, _):
            side, t = n // 8, n % 8
            tile_work(i, 1 + 5 * side, t, False)
            return 0

        lax.fori_loop(0, 16, outer_planes, 0)

        def inner_planes(n, _):
            tile_work(i, 2 + n // 8, n % 8, True)
            return 0

        lax.fori_loop(0, 8 * PLANES, inner_planes, 0)

        def edges(q, _):
            y_edges(i, q)
            return 0

        lax.fori_loop(0, PLANES, edges, 0)

        def collect(n, _):
            q, t = n // 8, n % 8
            r = pl.multiple_of(t * 8, 8)
            for out, x_flux, y_flux in ((out_f, tx, ty), (out_a, fx, fy)):
                for j in range(3):
                    d_x = x_flux[j, q + 3, pl.ds(r, 8), :] - x_flux[j, q + 1, pl.ds(r, 8), :]
                    d_y = y_flux[j, q, pl.ds(r + TOP + 1, 8), :] - y_flux[j, q, pl.ds(r + TOP - 1, 8), :]
                    out[i, j, q, pl.ds(r, 8), :] = out[i, j, q, pl.ds(r, 8), :] - d_x - d_y
            return 0

        lax.fori_loop(0, 8 * PLANES, collect, 0)
        return 0

    lax.fori_loop(0, insts, instance, 0)


def stencil(inflow, flow, adj, low, high, density, mask, labels):
    insts = flow.shape[0]
    shape = jax.ShapeDtypeStruct(flow.shape, jnp.float32)
    whole = pl.BlockSpec(memory_space=pltpu.VMEM)
    anywhere = pl.BlockSpec(memory_space=pl.ANY)
    return pl.pallas_call(
        stencil_kernel,
        out_shape=(shape, shape),
        in_specs=[pl.BlockSpec(memory_space=pltpu.SMEM)] + [anywhere] * 4 + [whole] * 3,
        out_specs=(whole, whole),
        scratch_shapes=[
            pltpu.VMEM((insts, 8, 8, PADDED, LANES), jnp.float32),
            pltpu.VMEM((3, 8, ROWS, LANES), jnp.float32),
            pltpu.VMEM((3, 8, ROWS, LANES), jnp.float32),
            pltpu.VMEM((3, PLANES, PADDED, LANES), jnp.float32),
            pltpu.VMEM((3, PLANES, PADDED, LANES), jnp.float32),
            pltpu.SemaphoreType.DMA((18,)),
        ],
        compiler_params=pltpu.CompilerParams(vmem_limit_bytes=40 << 20),
        cost_estimate=pl.CostEstimate(flops=40_000_000, bytes_accessed=8_000_000, transcendentals=400_000),
        name="stencil",
    )(inflow, flow, adj, low, high, density, mask, labels)


def spectral_row():
    k = np.arange(1, 8)
    return [float(v) for v in TIME_SCALE * 0.5 * np.where(k % 2 == 0, 1.0, -1.0) / np.tan(np.pi * k / NT)]


def time_kernel(x_ref, out_ref):
    coef = spectral_row()
    comps, planes = x_ref.shape[1:3]

    def step(n, _):
        c, q = n // planes, n % planes
        x = [x_ref[m, c, q] for m in range(NT)]
        sign = jnp.where(c < comps // 2, 1.0, -1.0)
        for n0 in range(NT // 2):
            diff = [(x[(n0 - k) % NT] - x[(n0 + k) % NT]) * sign for k in range(1, 8)]
            out_ref[n0, c, q] = sum(coef[k - 1] * diff[k - 1] for k in range(1, 8))
            out_ref[n0 + 8, c, q] = -sum(coef[k - 1] * diff[7 - k] for k in range(1, 8))
        return 0

    lax.fori_loop(0, comps * planes, step, 0)


def time_derivative(x):
    return pl.pallas_call(
        time_kernel,
        out_shape=jax.ShapeDtypeStruct(x.shape, jnp.float32),
        in_specs=[pl.BlockSpec(memory_space=pltpu.VMEM)],
        out_specs=pl.BlockSpec(memory_space=pltpu.VMEM),
        compiler_params=pltpu.CompilerParams(vmem_limit_bytes=16 << 20),
        name="time_derivative",
    )(x)


def add_kernel(f_ref, a_ref, t_ref, out_f, out_a):
    blocks, insts = t_ref.shape[:2]
    for base, source, out in ((0, f_ref, out_f), (3, a_ref, out_a)):
        for i in range(insts):
            for j in range(3):
                for b in range(blocks):
                    out[i, j, :, 8 * b : 8 * b + 8, :] = source[i, j, :, 8 * b : 8 * b + 8, :] + t_ref[b, i, base + j]
            out[i, 3] = source[i, 3]


def add_time(flow_part, adj_part, time_part):
    whole = pl.BlockSpec(memory_space=pltpu.VMEM)
    shape = jax.ShapeDtypeStruct(flow_part.shape, jnp.float32)
    return pl.pallas_call(
        add_kernel,
        out_shape=(shape, shape),
        in_specs=[whole] * 3,
        out_specs=(whole, whole),
        compiler_params=pltpu.CompilerParams(vmem_limit_bytes=24 << 20),
        name="add_time",
    )(flow_part, adj_part, time_part)


def boundary(flow, adj, planes, near):
    insts = flow.shape[0]
    far = jnp.concatenate([flow[:, :3, planes], adj[:, :3, planes]], axis=1)
    last = jnp.stack([flow[:, 3, near], adj[:, 3, near]], axis=1)
    return jnp.concatenate([far.reshape(insts, 12, ROWS, LANES), last], axis=1)


def on_device(flow, adj, density, mask, labels):
    insts = flow.shape[0]
    times = lax.axis_size("tm")
    count = lax.axis_size("space")
    instances = lax.axis_index("tm") * insts + jnp.arange(insts, dtype=jnp.int32)
    inflow = 1.0 + 0.5 * jnp.sin(2.0 * jnp.pi * instances.astype(jnp.float32) / NT)

    low = lax.ppermute(
        boundary(flow, adj, slice(PLANES - 2, PLANES), PLANES - 1), "space", [(i, i + 1) for i in range(count - 1)]
    )
    high = lax.ppermute(boundary(flow, adj, slice(0, 2), 0), "space", [(i + 1, i) for i in range(count - 1)])

    both = jnp.concatenate([flow[:, :3], adj[:, :3]], axis=1)
    both = both.reshape(insts, 6, PLANES, times, ROWS // times, LANES).transpose(3, 0, 1, 2, 4, 5)
    gathered = lax.all_to_all(both, "tm", 0, 0, tiled=True)
    derived = time_derivative(gathered.reshape(NT, 6, PLANES, ROWS // times, LANES))
    derived = derived.reshape(times, insts, 6, PLANES, ROWS // times, LANES)
    time_part = lax.all_to_all(derived, "tm", 0, 0, tiled=True)

    flow_part, adj_part = stencil(inflow, flow, adj, low, high, density, mask, labels)
    return add_time(flow_part, adj_part, time_part)


def solution(mesh):
    split = P("tm", None, "space", None, None)
    cells = P("space", None, None)
    return jax.shard_map(
        on_device,
        mesh=mesh,
        in_specs=(split, split, cells, cells, cells),
        out_specs=(split, split),
        check_vma=False,
    )
```

```python
import functools

import jax
import jax.numpy as jnp
from jax import lax
from jax.experimental import pallas as pl
from jax.experimental.pallas import tpu as pltpu
from jax.sharding import PartitionSpec as P
import numpy as np

NT = 16
NU_INF = 0.0616
NU_ZERO = 1.0
LAMBDA_SQ = 3.313 * 3.313
POWER = (0.3568 - 1.0) / 2.0
BRINKMAN_MAX = 8.0
RAMP_SHAPE = 0.1
TIME_SCALE = 0.25

PLANES = 4
ROWS = 64
LANES = 128
TOP = 8
PADDED = ROWS + 2 * TOP
TILE = 16
UNROLL = 2
VMEM_LIMIT = 56 << 20
EARLY_COST = 40_000_000_000
LATE_COST = 40_000_000_000
ADD_LIMIT = 12 << 20

MU_A = 0.25 * NU_INF
MU_B = 0.25 * (NU_ZERO - NU_INF)
SHEAR = LAMBDA_SQ / 8.0
DMU = (NU_ZERO - NU_INF) * POWER * LAMBDA_SQ / 16.0


def viscosity(square_sum):
    q = 1.0 + SHEAR * square_sum
    log_q = jnp.log(q)
    return MU_A + MU_B * jnp.exp(POWER * log_q), DMU * jnp.exp((POWER - 1.0) * log_q)


def outer_cell(u, lam, axis):
    strain = [u[j] + u[j] if j == axis else u[j] for j in range(3)]
    rate = [lam[j] + lam[j] if j == axis else lam[j] for j in range(3)]
    others = [j for j in range(3) if j != axis]
    square = sum(strain[j] * strain[j] for j in others)
    cross = sum(strain[j] * rate[j] for j in others)
    square = square + square + strain[axis] * strain[axis]
    cross = cross + cross + strain[axis] * rate[axis]
    mu, dmu = viscosity(square)
    slope = dmu * cross
    return [mu * s for s in strain], [mu * e + slope * s for s, e in zip(strain, rate)]


def stencil_tools(inflow_ref, w, tx, fx, ty, fy, out_f, out_a, density_ref, mask_ref, labels_ref):
    lane = lax.broadcasted_iota(jnp.int32, (TILE, LANES), 1)
    is_first = lane == 0
    is_last = lane == LANES - 1

    def along_z(f):
        up = jnp.where(is_last, 0.0, pltpu.roll(f, LANES - 1, 1))
        down = jnp.where(is_first, 0.0, pltpu.roll(f, 1, 1))
        return up - down

    def along_z_outer(f, outer):
        up = jnp.where(is_last, -outer, pltpu.roll(f, LANES - 1, 1))
        down = jnp.where(is_first, outer, pltpu.roll(f, 1, 1))
        return up - down

    def tile_work(i, p, t, interior):
        r = TOP + pl.multiple_of(t * TILE, 8)
        here = pl.ds(r, TILE)
        u = [w[i, j, p, here, :] for j in range(3)]
        lam = [w[i, 3 + j, p, here, :] for j in range(3)]
        grads, rates = [], []
        for base, values, into in ((0, u, grads), (3, lam, rates)):
            into.append([w[i, base + j, p + 1, here, :] - w[i, base + j, p - 1, here, :] for j in range(3)])
            into.append(
                [w[i, base + j, p, pl.ds(r + 1, TILE), :] - w[i, base + j, p, pl.ds(r - 1, TILE), :] for j in range(3)]
            )
            into.append([along_z(v) for v in values])
        strain = [[grads[k][j] + grads[j][k] for k in range(3)] for j in range(3)]
        rate = [[rates[k][j] + rates[j][k] for k in range(3)] for j in range(3)]
        pairs = ((0, 1), (0, 2), (1, 2))
        square = sum(strain[j][k] * strain[j][k] for j, k in pairs)
        cross = sum(strain[j][k] * rate[j][k] for j, k in pairs)
        square = square + square + sum(strain[j][j] * strain[j][j] for j in range(3))
        cross = cross + cross + sum(strain[j][j] * rate[j][j] for j in range(3))
        mu, dmu = viscosity(square)
        slope = dmu * cross
        half_u = [0.5 * v for v in u]
        half_p = 0.5 * w[i, 6, p, here, :]
        half_q = 0.5 * w[i, 7, p, here, :]

        def flux(j, k):
            t_jk = mu * strain[j][k]
            f_jk = mu * rate[j][k] + slope * strain[j][k] + half_u[k] * lam[j]
            if j == k:
                t_jk, f_jk = t_jk - half_p, f_jk + half_q
            return t_jk, f_jk

        for j in range(3):
            t_jk, f_jk = flux(j, 0)
            tx[i, j, p, pl.ds(r - TOP, TILE), :] = t_jk
            fx[i, j, p, pl.ds(r - TOP, TILE), :] = f_jk
        if not interior:
            return
        q = p - 2
        out_rows = pl.ds(r - TOP, TILE)
        for j in range(3):
            t_jk, f_jk = flux(j, 1)
            ty[j, q, here, :] = t_jk
            fy[j, q, here, :] = f_jk
        outer_t, outer_f = outer_cell(u, lam, 2)
        design = jnp.where(mask_ref[q, out_rows, :] == 1, density_ref[q, out_rows, :], 1.0)
        label = labels_ref[q, out_rows, :]
        ramp = (BRINKMAN_MAX * RAMP_SHAPE) * (1.0 - design) / (RAMP_SHAPE + design)
        penalty = jnp.where(label == 0, ramp, BRINKMAN_MAX)
        target = jnp.where(label == 2, inflow_ref[i], 0.0)
        half_lam = [0.5 * v for v in lam]
        for j in range(3):
            t_jk, f_jk = flux(j, 2)
            shifted = u[j] - target if j == 0 else u[j]
            out_f[i, j, q, out_rows, :] = (
                sum(half_u[k] * grads[k][j] for k in range(3)) - along_z_outer(t_jk, outer_t[j]) + penalty * shifted
            )
            out_a[i, j, q, out_rows, :] = (
                sum(half_lam[k] * grads[j][k] for k in range(3)) - along_z_outer(f_jk, outer_f[j]) + penalty * lam[j]
            )
        out_f[i, 3, q, out_rows, :] = 0.25 * (strain[0][0] + strain[1][1] + strain[2][2])
        out_a[i, 3, q, out_rows, :] = -0.25 * (rate[0][0] + rate[1][1] + rate[2][2])

    def y_edges(i, q):
        p = q + 2
        for first, keep, row, sign in ((TOP, 0, TOP - 1, 1.0), (TOP + ROWS - 8, 7, TOP + ROWS, -1.0)):
            u = [w[i, j, p, first : first + 8, :] for j in range(3)]
            lam = [w[i, 3 + j, p, first : first + 8, :] for j in range(3)]
            outer_t, outer_f = outer_cell(u, lam, 1)
            for j in range(3):
                ty[j, q, row : row + 1, :] = sign * outer_t[j][keep : keep + 1]
                fy[j, q, row : row + 1, :] = sign * outer_f[j][keep : keep + 1]

    def collect(i, p, t, with_x, with_y):
        q = p - 2
        r = pl.multiple_of(t * TILE, 8)
        for out, x_flux, y_flux in ((out_f, tx, ty), (out_a, fx, fy)):
            for j in range(3):
                total = out[i, j, q, pl.ds(r, TILE), :]
                if with_x:
                    total -= x_flux[i, j, p + 1, pl.ds(r, TILE), :] - x_flux[i, j, p - 1, pl.ds(r, TILE), :]
                if with_y:
                    total -= (
                        y_flux[j, q, pl.ds(r + TOP + 1, TILE), :] - y_flux[j, q, pl.ds(r + TOP - 1, TILE), :]
                    )
                out[i, j, q, pl.ds(r, TILE), :] = total

    def over(first, planes, work):
        tiles = ROWS // TILE

        def step(n, _):
            work(first + n // tiles, n % tiles)
            return 0

        lax.fori_loop(0, planes * tiles, step, 0, unroll=UNROLL)

    return tile_work, y_edges, collect, over


def clear_edges(w, i, first, planes):
    zero = jnp.zeros((TOP, LANES), jnp.float32)

    def clear(p, _):
        for c in range(6):
            w[i, c, first + p, 0:TOP, :] = zero
            w[i, c, first + p, TOP + ROWS : PADDED, :] = zero
        return 0

    lax.fori_loop(0, planes, clear, 0)


def early_kernel(
    core_ref, inflow_ref, flow_ref, adj_ref, halo_ref, density_hbm, mask_hbm, labels_hbm,
    flow_out, adj_out, tx_out, fx_out,
    out_f, out_a, density_ref, mask_ref, labels_ref, w, tx, fx, ty, fy, sems, cell_sems, out_sems,
):
    insts = out_f.shape[0]
    core = core_ref[0]
    data = pl.ds(TOP, ROWS)
    reads, writes = [], []
    three = pl.ds(1 - core, 3)
    for i in range(insts):
        copies = []
        for source, base, last in ((flow_ref, 0, 6), (adj_ref, 3, 7)):
            copies.append((source.at[i, 0:3], w.at[i, base : base + 3, 2:6, data, :]))
            copies.append((source.at[i, 3], w.at[i, last, 2:6, data, :]))
        for c in range(6):
            copies.append((halo_ref.at[i, 2 * c : 2 * c + 2], w.at[i, c, pl.ds(6 - 6 * core, 2), data, :]))
        copies.append((halo_ref.at[i, 12:14], w.at[i, 6:8, 6 - 5 * core, data, :]))
        reads.append([pltpu.make_async_copy(a, b, sems.at[i, k]) for k, (a, b) in enumerate(copies)])
        copies = [(a.at[i, :, three], b.at[i, :, three]) for a, b in ((out_f, flow_out), (out_a, adj_out))]
        copies += [(a.at[i, :, 3:5], b.at[i]) for a, b in ((tx, tx_out), (fx, fx_out))]
        writes.append([pltpu.make_async_copy(a, b, out_sems.at[i, k]) for k, (a, b) in enumerate(copies)])
    cells = ((density_hbm, density_ref), (mask_hbm, mask_ref), (labels_hbm, labels_ref))
    reads[0] += [pltpu.make_async_copy(a, b, cell_sems.at[k]) for k, (a, b) in enumerate(cells)]
    for group in reads:
        for h in group:
            h.start()
    for i in range(insts):
        clear_edges(w, i, 0, 8)
    tile_work, y_edges, collect, over = stencil_tools(
        inflow_ref, w, tx, fx, ty, fy, out_f, out_a, density_ref, mask_ref, labels_ref
    )
    for i in range(insts):
        for h in reads[i]:
            h.wait()
        over(6 - 5 * core, 1, lambda p, t: tile_work(i, p, t, False))
        over(3 - core, 3, lambda p, t: tile_work(i, p, t, True))

        def edges(n, _):
            y_edges(i, 1 - core + n)
            return 0

        lax.fori_loop(0, 3, edges, 0)
        over(4 - 2 * core, 2, lambda p, t: collect(i, p, t, True, True))
        over(3 + core, 1, lambda p, t: collect(i, p, t, False, True))
        for h in writes[i]:
            h.start()
    for group in writes:
        for h in group:
            h.wait()


def late_kernel(
    core_ref, inflow_ref, flow_ref, adj_ref, far_ref, last_ref, density_hbm, mask_hbm, labels_hbm,
    flow_part, adj_part, tx_part, fx_part, flow_out, adj_out,
    out_f, out_a, density_ref, mask_ref, labels_ref, w, tx, fx, ty, fy, sems, part_sems, cell_sems, out_sems,
):
    insts = out_f.shape[0]
    core = core_ref[0]
    data = pl.ds(TOP, ROWS)
    reads, parts, writes = [], [], []
    pair, partial = pl.ds(2 * core, 2), pl.ds(1 + core, 1)
    for i in range(insts):
        copies = []
        for source, base, last in ((flow_ref, 0, 6), (adj_ref, 3, 7)):
            copies.append((source.at[i, 0:3, pair], w.at[i, base : base + 3, pl.ds(2 + 2 * core, 2), data, :]))
            copies.append((source.at[i, 3, pair], w.at[i, last, pl.ds(2 + 2 * core, 2), data, :]))
        cut = far_ref.shape[0]
        halo_ref = far_ref.at[i] if i < cut else last_ref.at[i - cut]
        for c in range(6):
            copies.append((halo_ref.at[2 * c : 2 * c + 2], w.at[i, c, pl.ds(6 * core, 2), data, :]))
        copies.append((halo_ref.at[12:14], w.at[i, 6:8, 1 + 5 * core, data, :]))
        reads.append([pltpu.make_async_copy(a, b, sems.at[i, k]) for k, (a, b) in enumerate(copies)])
        copies = [(a.at[i, :, partial], b.at[i, :, partial]) for a, b in ((flow_out, out_f), (adj_out, out_a))]
        copies += [(a.at[i], b.at[i, :, 3:5]) for a, b in ((tx_part, tx), (fx_part, fx))]
        parts.append([pltpu.make_async_copy(a, b, part_sems.at[i, k]) for k, (a, b) in enumerate(copies)])
        copies = ((out_f, flow_out), (out_a, adj_out))
        writes.append([pltpu.make_async_copy(a.at[i, :, pair], b.at[i, :, pair], out_sems.at[i, k]) for k, (a, b) in enumerate(copies)])
    cells = ((density_hbm, density_ref), (mask_hbm, mask_ref), (labels_hbm, labels_ref))
    reads[0] += [
        pltpu.make_async_copy(a.at[pl.ds(3 * core, 1)], b.at[pl.ds(3 * core, 1)], cell_sems.at[k])
        for k, (a, b) in enumerate(cells)
    ]
    for i in range(insts):
        for h in reads[i] + parts[i]:
            h.start()
    for i in range(insts):
        clear_edges(w, i, 4 * core, 4)
    tile_work, y_edges, collect, over = stencil_tools(
        inflow_ref, w, tx, fx, ty, fy, out_f, out_a, density_ref, mask_ref, labels_ref
    )
    for i in range(insts):
        for h in reads[i]:
            h.wait()
        over(1 + 5 * core, 1, lambda p, t: tile_work(i, p, t, False))
        over(2 + 3 * core, 1, lambda p, t: tile_work(i, p, t, True))
        y_edges(i, 3 * core)
        for h in parts[i]:
            h.wait()
        over(2 + 3 * core, 1, lambda p, t: collect(i, p, t, True, True))
        over(3 + core, 1, lambda p, t: collect(i, p, t, True, False))
        for h in writes[i]:
            h.start()
    for group in writes:
        for h in group:
            h.wait()


def add_kernel(f_ref, a_ref, times, out_f, out_a, total, sems):
    insts = out_f.shape[0]
    work = [(i, n) for i in range(insts) for n in range(2)]
    reads, writes = [], []
    for k, (i, n) in enumerate(work):
        out = (out_f, out_a)[n].at[i, 0:3]
        reads.append(pltpu.make_async_copy(out, total.at[i, n], sems.at[0, k]))
        writes.append(pltpu.make_async_copy(total.at[i, n], out, sems.at[1, k]))
    for read in reads:
        read.start()
    for (i, n), read, write in zip(work, reads, writes):
        read.wait()
        for j in range(3):
            for b in range(2 * PLANES):
                q, rows = block_cells(b)
                total[i, n, j, q, rows, :] = total[i, n, j, q, rows, :] + times[b, i, 3 * n + j]
        write.start()
    for write in writes:
        write.wait()


def add_time(flow_part, adj_part, time_part):
    space = pl.BlockSpec(memory_space=pltpu.HBM)
    insts = flow_part.shape[0]
    shape = jax.ShapeDtypeStruct(flow_part.shape, jnp.float32)
    return pl.pallas_call(
        add_kernel,
        out_shape=(shape, shape),
        in_specs=[space] * 2 + [pl.BlockSpec(memory_space=pltpu.VMEM)],
        out_specs=[space] * 2,
        scratch_shapes=[
            pltpu.VMEM((insts, 2, 3) + flow_part.shape[2:], jnp.float32),
            pltpu.SemaphoreType.DMA((2, 2 * insts)),
        ],
        compiler_params=pltpu.CompilerParams(vmem_limit_bytes=ADD_LIMIT),
        input_output_aliases={0: 0, 1: 1},
        name="add_time",
    )(flow_part, adj_part, time_part)


def stencil(kernel, name, cost, out_shapes, core, inflow, flow, adj, halos, cells, *parts):
    insts = flow.shape[0]
    space = pl.BlockSpec(memory_space=pltpu.HBM)
    scalar = pl.BlockSpec(memory_space=pltpu.SMEM)
    like = lambda a: pltpu.VMEM(a.shape, a.dtype)
    late = len(parts) > 0
    return pl.pallas_call(
        kernel,
        out_shape=[jax.ShapeDtypeStruct(s, jnp.float32) for s in out_shapes],
        in_specs=[scalar] * 2 + [space] * (2 + len(halos) + len(cells) + len(parts)),
        out_specs=[space] * len(out_shapes),
        scratch_shapes=[like(flow), like(flow)]
        + [like(a) for a in cells]
        + [pltpu.VMEM((insts, 8, 8, PADDED, LANES), jnp.float32)]
        + [pltpu.VMEM((insts, 3, 8, ROWS, LANES), jnp.float32)] * 2
        + [pltpu.VMEM((3, PLANES, PADDED, LANES), jnp.float32)] * 2
        + [pltpu.SemaphoreType.DMA((insts, 11))]
        + ([pltpu.SemaphoreType.DMA((insts, 4))] if late else [])
        + [pltpu.SemaphoreType.DMA((3,)), pltpu.SemaphoreType.DMA((insts, 4))],
        compiler_params=pltpu.CompilerParams(vmem_limit_bytes=VMEM_LIMIT),
        cost_estimate=pl.CostEstimate(flops=cost, bytes_accessed=8_000_000, transcendentals=400_000),
        input_output_aliases={5 + len(halos) + len(cells) - 1 + k: k for k in range(2)} if late else {},
        name=name,
    )(core, inflow, flow, adj, *halos, *cells, *parts)


def spectral_row():
    k = np.arange(1, 8)
    return [float(v) for v in TIME_SCALE * 0.5 * np.where(k % 2 == 0, 1.0, -1.0) / np.tan(np.pi * k / NT)]


def time_kernel(x_ref, sent_hbm, out_hbm, out_ref, sems):
    comps, tiles = x_ref.shape[1], x_ref.shape[2] // 8
    writes = [pltpu.make_async_copy(out_ref.at[:, c], out_hbm.at[:, c], sems.at[c]) for c in range(comps)]
    for c in range(comps):
        coef = [v if c < comps // 2 else -v for v in spectral_row()]

        def step(n, _):
            rows = pl.ds(pl.multiple_of(n * 8, 8), 8)
            x = [x_ref[m, c, rows, :] for m in range(NT)]
            for m in range(NT // 2):
                diff = [x[(m - k) % NT] - x[(m + k) % NT] for k in range(1, 8)]
                out_ref[m, c, rows, :] = sum(coef[k - 1] * diff[k - 1] for k in range(1, 8))
                out_ref[m + 8, c, rows, :] = -sum(coef[k - 1] * diff[7 - k] for k in range(1, 8))
            return 0

        lax.fori_loop(0, tiles, step, 0, unroll=2)
        writes[c].start()
    for h in writes:
        h.wait()


def time_derivative(x, sent):
    return pl.pallas_call(
        time_kernel,
        out_shape=jax.ShapeDtypeStruct(x.shape, jnp.float32),
        in_specs=[pl.BlockSpec(memory_space=pltpu.VMEM), pl.BlockSpec(memory_space=pltpu.HBM)],
        out_specs=pl.BlockSpec(memory_space=pltpu.HBM),
        scratch_shapes=[pltpu.VMEM(x.shape, jnp.float32), pltpu.SemaphoreType.DMA((x.shape[1],))],
        compiler_params=pltpu.CompilerParams(vmem_limit_bytes=8 << 20),
        cost_estimate=pl.CostEstimate(flops=12_000_000, bytes_accessed=3_200_000, transcendentals=0),
        input_output_aliases={1: 0},
        name="time_derivative",
    )(x, sent)


def block_cells(b):
    half = ROWS // 2
    return b // 2, slice(b % 2 * half, (b % 2 + 1) * half)


def halo_copies(flow_ref, adj_ref, ref, insts, first, near):
    copies = []
    for j in range(3):
        copies.append((flow_ref.at[insts, j, pl.ds(first, 2)], ref.at[:, 2 * j : 2 * j + 2]))
        copies.append((adj_ref.at[insts, j, pl.ds(first, 2)], ref.at[:, 6 + 2 * j : 8 + 2 * j]))
    copies.append((flow_ref.at[insts, 3, pl.ds(near, 1)], ref.at[:, 12:13]))
    copies.append((adj_ref.at[insts, 3, pl.ds(near, 1)], ref.at[:, 13:14]))
    return copies


def block_copies(flow_ref, adj_ref, ref, b):
    q, rows = block_cells(b)
    return [(flow_ref.at[:, 0:3, q, rows], ref.at[b, :, 0:3]), (adj_ref.at[:, 0:3, q, rows], ref.at[b, :, 3:6])]


def through_vmem(groups, sems):
    flat = [c for copies, _ in groups for c in copies] + [write for _, write in groups]
    handles = [pltpu.make_async_copy(a, b, sems.at[i]) for i, (a, b) in enumerate(flat)]
    writes = handles[len(handles) - len(groups) :]
    for h in handles[: len(handles) - len(groups)]:
        h.start()
    done = 0
    for (copies, _), write in zip(groups, writes):
        for h in handles[done : done + len(copies)]:
            h.wait()
        done += len(copies)
        write.start()
    for write in writes:
        write.wait()


def pack_halo_kernel(core_ref, flow_ref, adj_ref, far_ref, last_ref, near_ref, far, last, near, sems):
    core = core_ref[0]
    insts = flow_ref.shape[0]
    cut = far.shape[0]
    groups = [(halo_copies(flow_ref, adj_ref, near, slice(0, insts), 2 - 2 * core, 3 - 3 * core), (near, near_ref))]
    for ref, out, which in ((far, far_ref, slice(0, cut)), (last, last_ref, slice(cut, insts))):
        groups.append((halo_copies(flow_ref, adj_ref, ref, which, 2 * core, 3 * core), (ref, out)))
    through_vmem(groups, sems)


def pack_block_kernel(core_ref, flow_ref, adj_ref, blocks_ref, blocks, sems):
    groups = [
        (block_copies(flow_ref, adj_ref, blocks, b), (blocks.at[b], blocks_ref.at[b])) for b in range(2 * PLANES)
    ]
    through_vmem(groups, sems)


def pack(kernel, name, core, flow, adj, shapes):
    space = pl.BlockSpec(memory_space=pltpu.HBM)
    return pl.pallas_call(
        kernel,
        out_shape=[jax.ShapeDtypeStruct(s, jnp.float32) for s in shapes],
        in_specs=[pl.BlockSpec(memory_space=pltpu.SMEM)] + [space] * 2,
        out_specs=[space] * len(shapes),
        scratch_shapes=[pltpu.VMEM(s, jnp.float32) for s in shapes] + [pltpu.SemaphoreType.DMA((7 * PLANES,))],
        compiler_params=pltpu.CompilerParams(vmem_limit_bytes=VMEM_LIMIT),
        name=name,
    )(core, flow, adj)


def on_device(flow, adj, density, mask, labels):
    insts = flow.shape[0]
    count = lax.axis_size("space")
    instances = lax.axis_index("tm") * insts + jnp.arange(insts, dtype=jnp.int32)
    inflow = 1.0 + 0.5 * jnp.sin(2.0 * jnp.pi * instances.astype(jnp.float32) / NT)

    core = lax.axis_index("space") % 2
    core = core.reshape(1)
    halo = (insts, 14, ROWS, LANES)
    cut = insts // 2
    halves = [(cut,) + halo[1:], (insts - cut,) + halo[1:]]
    far, last, near = pack(pack_halo_kernel, "pack_halo", core, flow, adj, halves + [halo])
    across = [p for i in range(1, count - 1, 2) for p in ((i, i + 1), (i + 1, i))]
    far, last = lax.ppermute(far, "space", across), lax.ppermute(last, "space", across)
    near = lax.ppermute(near, "space", [p for i in range(0, count, 2) for p in ((i, i + 1), (i + 1, i))])
    (blocks,) = pack(pack_block_kernel, "pack_block", core, flow, adj, [(2 * PLANES, insts, 6, ROWS // 2, LANES)])
    gathered = lax.all_to_all(blocks, "tm", 0, 0, tiled=True)
    cells = (density, mask, labels)
    edge = (insts, 3, 2, ROWS, LANES)
    parts = stencil(
        early_kernel, "early", EARLY_COST, [flow.shape] * 2 + [edge] * 2, core, inflow, flow, adj, [near], cells
    )
    gathered, *parts = lax.optimization_barrier((gathered, *parts))
    by_time = (NT,) + blocks.shape[2:]
    derived = time_derivative(gathered.reshape(by_time), blocks.reshape(by_time))
    time_part = lax.all_to_all(derived.reshape(blocks.shape), "tm", 0, 0, tiled=True)
    late = stencil(late_kernel, "late", LATE_COST, [flow.shape] * 2, core, inflow, flow, adj, [far, last], cells, *parts)
    return add_time(*late, time_part)


def solution(mesh):
    split = P("tm", None, "space", None, None)
    cells = P("space", None, None)
    return jax.shard_map(
        on_device,
        mesh=mesh,
        in_specs=(split, split, cells, cells, cells),
        out_specs=(split, split),
        check_vma=False,
    )
```

```python
import functools

import jax
import jax.numpy as jnp
from jax import lax
from jax.experimental import pallas as pl
from jax.experimental.pallas import tpu as pltpu
from jax.sharding import PartitionSpec as P
import numpy as np

NT = 16
NU_INF = 0.0616
NU_ZERO = 1.0
LAMBDA_SQ = 3.313 * 3.313
POWER = (0.3568 - 1.0) / 2.0
BRINKMAN_MAX = 8.0
RAMP_SHAPE = 0.1
TIME_SCALE = 0.25

PLANES = 4
ROWS = 64
LANES = 128
TOP = 8
PADDED = ROWS + 2 * TOP
TILE = 16
UNROLL = 2
VMEM_LIMIT = 56 << 20
EARLY_COST = 20_000_000_000
LATE_COST = 40_000_000_000
ADD_LIMIT = 12 << 20
GATED = False

MU_A = 0.25 * NU_INF
MU_B = 0.25 * (NU_ZERO - NU_INF)
SHEAR = LAMBDA_SQ / 8.0
DMU = (NU_ZERO - NU_INF) * POWER * LAMBDA_SQ / 16.0


def viscosity(square_sum):
    q = 1.0 + SHEAR * square_sum
    log_q = jnp.log(q)
    return MU_A + MU_B * jnp.exp(POWER * log_q), DMU * jnp.exp((POWER - 1.0) * log_q)


def outer_cell(u, lam, axis):
    strain = [u[j] + u[j] if j == axis else u[j] for j in range(3)]
    rate = [lam[j] + lam[j] if j == axis else lam[j] for j in range(3)]
    others = [j for j in range(3) if j != axis]
    square = sum(strain[j] * strain[j] for j in others)
    cross = sum(strain[j] * rate[j] for j in others)
    square = square + square + strain[axis] * strain[axis]
    cross = cross + cross + strain[axis] * rate[axis]
    mu, dmu = viscosity(square)
    slope = dmu * cross
    return [mu * s for s in strain], [mu * e + slope * s for s, e in zip(strain, rate)]


def stencil_tools(inflow_ref, w, tx, fx, ty, fy, out_f, out_a, density_ref, mask_ref, labels_ref):
    lane = lax.broadcasted_iota(jnp.int32, (TILE, LANES), 1)
    is_first = lane == 0
    is_last = lane == LANES - 1

    def along_z(f):
        up = jnp.where(is_last, 0.0, pltpu.roll(f, LANES - 1, 1))
        down = jnp.where(is_first, 0.0, pltpu.roll(f, 1, 1))
        return up - down

    def along_z_outer(f, outer):
        up = jnp.where(is_last, -outer, pltpu.roll(f, LANES - 1, 1))
        down = jnp.where(is_first, outer, pltpu.roll(f, 1, 1))
        return up - down

    def tile_work(i, p, t, interior):
        r = TOP + pl.multiple_of(t * TILE, 8)
        here = pl.ds(r, TILE)
        u = [w[i, j, p, here, :] for j in range(3)]
        lam = [w[i, 3 + j, p, here, :] for j in range(3)]
        grads, rates = [], []
        for base, values, into in ((0, u, grads), (3, lam, rates)):
            into.append([w[i, base + j, p + 1, here, :] - w[i, base + j, p - 1, here, :] for j in range(3)])
            into.append(
                [w[i, base + j, p, pl.ds(r + 1, TILE), :] - w[i, base + j, p, pl.ds(r - 1, TILE), :] for j in range(3)]
            )
            into.append([along_z(v) for v in values])
        strain = [[grads[k][j] + grads[j][k] for k in range(3)] for j in range(3)]
        rate = [[rates[k][j] + rates[j][k] for k in range(3)] for j in range(3)]
        pairs = ((0, 1), (0, 2), (1, 2))
        square = sum(strain[j][k] * strain[j][k] for j, k in pairs)
        cross = sum(strain[j][k] * rate[j][k] for j, k in pairs)
        square = square + square + sum(strain[j][j] * strain[j][j] for j in range(3))
        cross = cross + cross + sum(strain[j][j] * rate[j][j] for j in range(3))
        mu, dmu = viscosity(square)
        slope = dmu * cross
        half_u = [0.5 * v for v in u]
        half_p = 0.5 * w[i, 6, p, here, :]
        half_q = 0.5 * w[i, 7, p, here, :]

        def flux(j, k):
            t_jk = mu * strain[j][k]
            f_jk = mu * rate[j][k] + slope * strain[j][k] + half_u[k] * lam[j]
            if j == k:
                t_jk, f_jk = t_jk - half_p, f_jk + half_q
            return t_jk, f_jk

        for j in range(3):
            t_jk, f_jk = flux(j, 0)
            tx[i, j, p, pl.ds(r - TOP, TILE), :] = t_jk
            fx[i, j, p, pl.ds(r - TOP, TILE), :] = f_jk
        if not interior:
            return
        q = p - 2
        out_rows = pl.ds(r - TOP, TILE)
        for j in range(3):
            t_jk, f_jk = flux(j, 1)
            ty[j, q, here, :] = t_jk
            fy[j, q, here, :] = f_jk
        outer_t, outer_f = outer_cell(u, lam, 2)
        design = jnp.where(mask_ref[q, out_rows, :] == 1, density_ref[q, out_rows, :], 1.0)
        label = labels_ref[q, out_rows, :]
        ramp = (BRINKMAN_MAX * RAMP_SHAPE) * (1.0 - design) / (RAMP_SHAPE + design)
        penalty = jnp.where(label == 0, ramp, BRINKMAN_MAX)
        target = jnp.where(label == 2, inflow_ref[i], 0.0)
        half_lam = [0.5 * v for v in lam]
        for j in range(3):
            t_jk, f_jk = flux(j, 2)
            shifted = u[j] - target if j == 0 else u[j]
            out_f[i, j, q, out_rows, :] = (
                sum(half_u[k] * grads[k][j] for k in range(3)) - along_z_outer(t_jk, outer_t[j]) + penalty * shifted
            )
            out_a[i, j, q, out_rows, :] = (
                sum(half_lam[k] * grads[j][k] for k in range(3)) - along_z_outer(f_jk, outer_f[j]) + penalty * lam[j]
            )
        out_f[i, 3, q, out_rows, :] = 0.25 * (strain[0][0] + strain[1][1] + strain[2][2])
        out_a[i, 3, q, out_rows, :] = -0.25 * (rate[0][0] + rate[1][1] + rate[2][2])

    def y_edges(i, q):
        p = q + 2
        for first, keep, row, sign in ((TOP, 0, TOP - 1, 1.0), (TOP + ROWS - 8, 7, TOP + ROWS, -1.0)):
            u = [w[i, j, p, first : first + 8, :] for j in range(3)]
            lam = [w[i, 3 + j, p, first : first + 8, :] for j in range(3)]
            outer_t, outer_f = outer_cell(u, lam, 1)
            for j in range(3):
                ty[j, q, row : row + 1, :] = sign * outer_t[j][keep : keep + 1]
                fy[j, q, row : row + 1, :] = sign * outer_f[j][keep : keep + 1]

    def collect(i, p, t, with_x, with_y):
        q = p - 2
        r = pl.multiple_of(t * TILE, 8)
        for out, x_flux, y_flux in ((out_f, tx, ty), (out_a, fx, fy)):
            for j in range(3):
                total = out[i, j, q, pl.ds(r, TILE), :]
                if with_x:
                    total -= x_flux[i, j, p + 1, pl.ds(r, TILE), :] - x_flux[i, j, p - 1, pl.ds(r, TILE), :]
                if with_y:
                    total -= (
                        y_flux[j, q, pl.ds(r + TOP + 1, TILE), :] - y_flux[j, q, pl.ds(r + TOP - 1, TILE), :]
                    )
                out[i, j, q, pl.ds(r, TILE), :] = total

    def over(first, planes, work):
        tiles = ROWS // TILE

        def step(n, _):
            work(first + n // tiles, n % tiles)
            return 0

        lax.fori_loop(0, planes * tiles, step, 0, unroll=UNROLL)

    return tile_work, y_edges, collect, over


def clear_edges(w, i, first, planes):
    zero = jnp.zeros((TOP, LANES), jnp.float32)

    def clear(p, _):
        for c in range(6):
            w[i, c, first + p, 0:TOP, :] = zero
            w[i, c, first + p, TOP + ROWS : PADDED, :] = zero
        return 0

    lax.fori_loop(0, planes, clear, 0)


def early_kernel(
    core_ref, inflow_ref, flow_ref, adj_ref, near_ref, density_hbm, mask_hbm, labels_hbm,
    flow_out, adj_out, tx_out, fx_out,
    out_f, out_a, density_ref, mask_ref, labels_ref, w, tx, fx, ty, fy, sems, cell_sems, out_sems,
):
    insts = out_f.shape[0]
    core = core_ref[0]
    data = pl.ds(TOP, ROWS)
    reads, writes = [], []
    three = pl.ds(1 - core, 3)
    for i in range(insts):
        copies = []
        for source, base, last in ((flow_ref, 0, 6), (adj_ref, 3, 7)):
            copies.append((source.at[i, 0:3], w.at[i, base : base + 3, 2:6, data, :]))
            copies.append((source.at[i, 3], w.at[i, last, 2:6, data, :]))
        for n in range(2):
            for j in range(3):
                copies.append((near_ref.at[i, n, 2 * j : 2 * j + 2], w.at[i, 3 * n + j, pl.ds(6 - 6 * core, 2), data, :]))
            copies.append((near_ref.at[i, n, 6], w.at[i, 6 + n, 6 - 5 * core, data, :]))
        reads.append([pltpu.make_async_copy(a, b, sems.at[i, k]) for k, (a, b) in enumerate(copies)])
        copies = [(a.at[i, :, three], b.at[i, :, three]) for a, b in ((out_f, flow_out), (out_a, adj_out))]
        copies += [(a.at[i, :, 3:5], b.at[i]) for a, b in ((tx, tx_out), (fx, fx_out))]
        writes.append([pltpu.make_async_copy(a, b, out_sems.at[i, k]) for k, (a, b) in enumerate(copies)])
    cells = ((density_hbm, density_ref), (mask_hbm, mask_ref), (labels_hbm, labels_ref))
    reads[0] += [pltpu.make_async_copy(a, b, cell_sems.at[k]) for k, (a, b) in enumerate(cells)]
    for group in reads:
        for h in group:
            h.start()
    for i in range(insts):
        clear_edges(w, i, 0, 8)
    tile_work, y_edges, collect, over = stencil_tools(
        inflow_ref, w, tx, fx, ty, fy, out_f, out_a, density_ref, mask_ref, labels_ref
    )
    for i in range(insts):
        for h in reads[i]:
            h.wait()
        over(6 - 5 * core, 1, lambda p, t: tile_work(i, p, t, False))
        over(3 - core, 3, lambda p, t: tile_work(i, p, t, True))

        def edges(n, _):
            y_edges(i, 1 - core + n)
            return 0

        lax.fori_loop(0, 3, edges, 0)
        over(4 - 2 * core, 2, lambda p, t: collect(i, p, t, True, True))
        over(3 + core, 1, lambda p, t: collect(i, p, t, False, True))
        for h in writes[i]:
            h.start()
    for group in writes:
        for h in group:
            h.wait()


def late_kernel(core_ref, inflow_ref, flow_ref, adj_ref, far_ref, *refs):
    cells_hbm, (_, _, tx_part, fx_part, flow_out, adj_out, sent), refs = refs[:3], refs[3:10], refs[10:]
    out_f, out_a, density_ref, mask_ref, labels_ref, w, tx, fx, ty, fy, sems, part_sems, cell_sems, out_sems = refs
    insts = out_f.shape[0]
    core = core_ref[0]
    at_end = inflow_ref[insts]
    data = pl.ds(TOP, ROWS)
    pair, partial, own = pl.ds(2 * core, 2), pl.ds(1 + core, 1), pl.ds(2 + 2 * core, 2)
    edge, last = 2 + 3 * core, 3 * core
    reads, parts, writes = [], [], []
    for i in range(insts):
        copies = []
        for n, source in enumerate((flow_ref, adj_ref)):
            vel = slice(3 * n, 3 * n + 3)
            copies.append((source.at[i, 0:3, pair], w.at[i, vel, own, data, :]))
            copies.append((source.at[i, 3, pair], w.at[i, 6 + n, own, data, :]))
            copies.append((far_ref.at[i, n], w.at[i, vel, 1 + 5 * core, data, :]))
        reads.append([pltpu.make_async_copy(a, b, sems.at[i, k]) for k, (a, b) in enumerate(copies)])
        copies = [(a.at[i, :, partial], b.at[i, :, partial]) for a, b in ((flow_out, out_f), (adj_out, out_a))]
        copies += [(a.at[i], b.at[i, :, 3:5]) for a, b in ((tx_part, tx), (fx_part, fx))]
        parts.append([pltpu.make_async_copy(a, b, part_sems.at[i, k]) for k, (a, b) in enumerate(copies)])
        copies = [(a.at[i, :, edge], sent.at[i, n]) for n, a in enumerate((tx, fx))]
        copies += [(a.at[i, :, pair], b.at[i, :, pair]) for a, b in ((out_f, flow_out), (out_a, adj_out))]
        writes.append([pltpu.make_async_copy(a, b, out_sems.at[i, k]) for k, (a, b) in enumerate(copies)])
    here = pl.ds(last, 1)
    cells = zip(cells_hbm, (density_ref, mask_ref, labels_ref))
    reads[0] += [pltpu.make_async_copy(a.at[here], b.at[here], cell_sems.at[k]) for k, (a, b) in enumerate(cells)]
    for i in range(insts):
        for h in reads[i] + parts[i]:
            h.start()
    for i in range(insts):
        clear_edges(w, i, 1 + 3 * core, 3)
    tile_work, y_edges, collect, over = stencil_tools(
        inflow_ref, w, tx, fx, ty, fy, out_f, out_a, density_ref, mask_ref, labels_ref
    )
    sign = at_end * (1.0 - 2.0 * core.astype(jnp.float32))

    def beyond(i, t):
        r = pl.multiple_of(t * TILE, 8)
        here = pl.ds(r + TOP, TILE)
        u = [w[i, j, edge, here, :] for j in range(3)]
        lam = [w[i, 3 + j, edge, here, :] for j in range(3)]
        outer_t, outer_f = outer_cell(u, lam, 0)
        for j in range(3):
            tx[i, j, 1 + 5 * core, pl.ds(r, TILE), :] = sign * outer_t[j]
            fx[i, j, 1 + 5 * core, pl.ds(r, TILE), :] = sign * outer_f[j]

    for i in range(insts):
        for h in reads[i]:
            h.wait()
        over(edge, 1, lambda p, t: tile_work(i, p, t, True))
        for h in writes[i][:2]:
            h.start()
        y_edges(i, last)
        over(edge, 1, lambda p, t: beyond(i, t))
        for h in parts[i]:
            h.wait()
        over(edge, 1, lambda p, t: collect(i, p, t, True, True))
        over(3 + core, 1, lambda p, t: collect(i, p, t, True, False))
        for h in writes[i][2:]:
            h.start()
    for group in writes:
        for h in group:
            h.wait()


def flux_kernel(core_ref, f_ref, a_ref, flux_hbm, out_f, out_a, total, flux, sems):
    insts = out_f.shape[0]
    core = core_ref[0]
    sign = 1.0 - 2.0 * core.astype(jnp.float32)
    work = [(i, n) for i in range(insts) for n in range(2)]
    reads, writes = [], []
    for k, (i, n) in enumerate(work):
        out = (out_f, out_a)[n].at[i, 0:3, 3 * core]
        reads.append(
            (
                pltpu.make_async_copy(out, total.at[i, n], sems.at[0, k]),
                pltpu.make_async_copy(flux_hbm.at[i, n], flux.at[i, n], sems.at[1, k]),
            )
        )
        writes.append(pltpu.make_async_copy(total.at[i, n], out, sems.at[2, k]))
    for read in reads:
        for h in read:
            h.start()
    for (i, n), read, write in zip(work, reads, writes):
        for h in read:
            h.wait()
        total[i, n] = total[i, n] + sign * flux[i, n]
        write.start()
    for write in writes:
        write.wait()


def add_flux(core, flow_part, adj_part, flux):
    space = pl.BlockSpec(memory_space=pltpu.HBM)
    shape = jax.ShapeDtypeStruct(flow_part.shape, jnp.float32)
    return pl.pallas_call(
        flux_kernel,
        out_shape=(shape, shape),
        in_specs=[pl.BlockSpec(memory_space=pltpu.SMEM)] + [space] * 3,
        out_specs=[space] * 2,
        scratch_shapes=[pltpu.VMEM(flux.shape, jnp.float32)] * 2
        + [pltpu.SemaphoreType.DMA((3, 2 * flow_part.shape[0]))],
        compiler_params=pltpu.CompilerParams(vmem_limit_bytes=VMEM_LIMIT),
        cost_estimate=pl.CostEstimate(flops=LATE_COST, bytes_accessed=8_000_000, transcendentals=0),
        input_output_aliases={1: 0, 2: 1},
        name="add_flux",
    )(core, flow_part, adj_part, flux)


def add_kernel(f_ref, a_ref, times, out_f, out_a, total, sems):
    insts = out_f.shape[0]
    work = [(i, n) for i in range(insts) for n in range(2)]
    reads, writes = [], []
    for k, (i, n) in enumerate(work):
        out = (out_f, out_a)[n].at[i, 0:3]
        reads.append(pltpu.make_async_copy(out, total.at[i, n], sems.at[0, k]))
        writes.append(pltpu.make_async_copy(total.at[i, n], out, sems.at[1, k]))
    for read in reads:
        read.start()
    for (i, n), read, write in zip(work, reads, writes):
        read.wait()
        for j in range(3):
            for b in range(2 * PLANES):
                q, rows = block_cells(b)
                total[i, n, j, q, rows, :] = total[i, n, j, q, rows, :] + times[b, i, 3 * n + j]
        write.start()
    for write in writes:
        write.wait()


def add_time(flow_part, adj_part, time_part):
    space = pl.BlockSpec(memory_space=pltpu.HBM)
    insts = flow_part.shape[0]
    shape = jax.ShapeDtypeStruct(flow_part.shape, jnp.float32)
    return pl.pallas_call(
        add_kernel,
        out_shape=(shape, shape),
        in_specs=[space] * 2 + [pl.BlockSpec(memory_space=pltpu.VMEM)],
        out_specs=[space] * 2,
        scratch_shapes=[
            pltpu.VMEM((insts, 2, 3) + flow_part.shape[2:], jnp.float32),
            pltpu.SemaphoreType.DMA((2, 2 * insts)),
        ],
        compiler_params=pltpu.CompilerParams(vmem_limit_bytes=ADD_LIMIT),
        input_output_aliases={0: 0, 1: 1},
        name="add_time",
    )(flow_part, adj_part, time_part)


def stencil(kernel, name, cost, out_shapes, core, inflow, flow, adj, halos, cells, *parts):
    insts = flow.shape[0]
    space = pl.BlockSpec(memory_space=pltpu.HBM)
    scalar = pl.BlockSpec(memory_space=pltpu.SMEM)
    like = lambda a: pltpu.VMEM(a.shape, a.dtype)
    late = len(parts) > 0
    return pl.pallas_call(
        kernel,
        out_shape=[jax.ShapeDtypeStruct(s, jnp.float32) for s in out_shapes],
        in_specs=[scalar] * 2 + [space] * (2 + len(halos) + len(cells) + len(parts)),
        out_specs=[space] * len(out_shapes),
        scratch_shapes=[like(flow), like(flow)]
        + [like(a) for a in cells]
        + [pltpu.VMEM((insts, 8, 8, PADDED, LANES), jnp.float32)]
        + [pltpu.VMEM((insts, 3, 8, ROWS, LANES), jnp.float32)] * 2
        + [pltpu.VMEM((3, PLANES, PADDED, LANES), jnp.float32)] * 2
        + [pltpu.SemaphoreType.DMA((insts, 12))]
        + ([pltpu.SemaphoreType.DMA((insts, 4))] if late else [])
        + [pltpu.SemaphoreType.DMA((3,)), pltpu.SemaphoreType.DMA((insts, 4))],
        compiler_params=pltpu.CompilerParams(vmem_limit_bytes=VMEM_LIMIT),
        cost_estimate=pl.CostEstimate(flops=cost, bytes_accessed=8_000_000, transcendentals=400_000),
        input_output_aliases={5 + len(halos) + len(cells) - 1 + k: k for k in range(2)} if late else {},
        name=name,
    )(core, inflow, flow, adj, *halos, *cells, *parts)


def spectral_row():
    k = np.arange(1, 8)
    return [float(v) for v in TIME_SCALE * 0.5 * np.where(k % 2 == 0, 1.0, -1.0) / np.tan(np.pi * k / NT)]


def time_kernel(x_ref, sent_hbm, out_hbm, out_ref, sems):
    comps, tiles = x_ref.shape[1], x_ref.shape[2] // 8
    writes = [pltpu.make_async_copy(out_ref.at[:, c], out_hbm.at[:, c], sems.at[c]) for c in range(comps)]
    for c in range(comps):
        coef = [v if c < comps // 2 else -v for v in spectral_row()]

        def step(n, _):
            rows = pl.ds(pl.multiple_of(n * 8, 8), 8)
            x = [x_ref[m, c, rows, :] for m in range(NT)]
            for m in range(NT // 2):
                diff = [x[(m - k) % NT] - x[(m + k) % NT] for k in range(1, 8)]
                out_ref[m, c, rows, :] = sum(coef[k - 1] * diff[k - 1] for k in range(1, 8))
                out_ref[m + 8, c, rows, :] = -sum(coef[k - 1] * diff[7 - k] for k in range(1, 8))
            return 0

        lax.fori_loop(0, tiles, step, 0, unroll=2)
        writes[c].start()
    for h in writes:
        h.wait()


def time_derivative(x, sent):
    return pl.pallas_call(
        time_kernel,
        out_shape=jax.ShapeDtypeStruct(x.shape, jnp.float32),
        in_specs=[pl.BlockSpec(memory_space=pltpu.VMEM), pl.BlockSpec(memory_space=pltpu.HBM)],
        out_specs=pl.BlockSpec(memory_space=pltpu.HBM),
        scratch_shapes=[pltpu.VMEM(x.shape, jnp.float32), pltpu.SemaphoreType.DMA((x.shape[1],))],
        compiler_params=pltpu.CompilerParams(vmem_limit_bytes=8 << 20),
        cost_estimate=pl.CostEstimate(flops=12_000_000, bytes_accessed=3_200_000, transcendentals=0),
        input_output_aliases={1: 0},
        name="time_derivative",
    )(x, sent)


def block_cells(b):
    half = ROWS // 2
    return b // 2, slice(b % 2 * half, (b % 2 + 1) * half)


def halo_copies(state_ref, ref, first, near):
    copies = [(state_ref.at[:, j, pl.ds(first, 2)], ref.at[:, 2 * j : 2 * j + 2]) for j in range(3)]
    return copies + [(state_ref.at[:, 3, pl.ds(near, 1)], ref.at[:, 6:7])]


def block_copies(flow_ref, adj_ref, ref, b):
    q, rows = block_cells(b)
    return [(flow_ref.at[:, 0:3, q, rows], ref.at[b, :, 0:3]), (adj_ref.at[:, 0:3, q, rows], ref.at[b, :, 3:6])]


def through_vmem(groups, sems):
    flat = [c for copies, _ in groups for c in copies] + [write for _, write in groups]
    handles = [pltpu.make_async_copy(a, b, sems.at[i]) for i, (a, b) in enumerate(flat)]
    writes = handles[len(handles) - len(groups) :]
    for h in handles[: len(handles) - len(groups)]:
        h.start()
    done = 0
    for (copies, _), write in zip(groups, writes):
        for h in handles[done : done + len(copies)]:
            h.wait()
        done += len(copies)
        write.start()
    for write in writes:
        write.wait()


def pack_kernel(core_ref, flow_ref, adj_ref, blocks_ref, near_ref, far_ref, blocks, near, far, sems):
    core = core_ref[0]
    states = (flow_ref, adj_ref)
    copies = sum([halo_copies(state, near.at[:, n], 2 - 2 * core, 3 - 3 * core) for n, state in enumerate(states)], [])
    halos = [(copies, (near, near_ref))]
    copies = [(state.at[:, 0:3, 3 * core], far.at[:, n]) for n, state in enumerate(states)]
    halos.append((copies, (far, far_ref)))
    groups = []
    for b in range(2 * PLANES):
        groups.append((block_copies(flow_ref, adj_ref, blocks, b), (blocks.at[b], blocks_ref.at[b])))
    through_vmem(halos + groups, sems)


def pack(core, flow, adj):
    insts = flow.shape[0]
    space = pl.BlockSpec(memory_space=pltpu.HBM)
    halo = (insts, 2, 7, ROWS, LANES)
    blocks = (2 * PLANES, insts, 6, ROWS // 2, LANES)
    shapes = [blocks, halo, (insts, 2, 3, ROWS, LANES)]
    copies = 8 + 1 + 2 + 1 + 6 * PLANES
    return pl.pallas_call(
        pack_kernel,
        out_shape=[jax.ShapeDtypeStruct(s, jnp.float32) for s in shapes],
        in_specs=[pl.BlockSpec(memory_space=pltpu.SMEM)] + [space] * 2,
        out_specs=[space] * len(shapes),
        scratch_shapes=[
            pltpu.VMEM(blocks, jnp.float32),
            pltpu.VMEM(halo, jnp.float32),
            pltpu.VMEM(shapes[2], jnp.float32),
            pltpu.SemaphoreType.DMA((copies,)),
        ],
        compiler_params=pltpu.CompilerParams(vmem_limit_bytes=VMEM_LIMIT),
        name="pack",
    )(core, flow, adj)


def on_device(flow, adj, density, mask, labels):
    insts = flow.shape[0]
    count = lax.axis_size("space")
    instances = lax.axis_index("tm") * insts + jnp.arange(insts, dtype=jnp.int32)
    inflow = 1.0 + 0.5 * jnp.sin(2.0 * jnp.pi * instances.astype(jnp.float32) / NT)

    core = lax.axis_index("space") % 2
    at_end = (lax.axis_index("space") == 0) | (lax.axis_index("space") == count - 1)
    core = core.reshape(1)
    scalars = jnp.append(inflow, at_end.astype(jnp.float32))
    blocks, near, far = pack(core, flow, adj)
    near = lax.ppermute(near, "space", [p for i in range(0, count, 2) for p in ((i, i + 1), (i + 1, i))])
    across = [p for i in range(1, count - 1, 2) for p in ((i, i + 1), (i + 1, i))]
    far = lax.ppermute(far, "space", across)
    if GATED:
        blocks, near = lax.optimization_barrier((blocks, near))
    gathered = lax.all_to_all(blocks, "tm", 0, 0, tiled=True)
    cells = (density, mask, labels)
    edge = (insts, 3, 2, ROWS, LANES)
    parts = stencil(
        early_kernel, "early", EARLY_COST, [flow.shape] * 2 + [edge] * 2, core, scalars, flow, adj, [near], cells
    )
    shapes = [flow.shape] * 2 + [(insts, 2, 3, ROWS, LANES)]
    *parts, flux = stencil(late_kernel, "late", LATE_COST, shapes, core, scalars, flow, adj, [far], cells, *parts)
    flux = lax.ppermute(flux, "space", across)
    gathered, *parts = lax.optimization_barrier((gathered, *parts))
    by_time = (NT,) + blocks.shape[2:]
    derived = time_derivative(gathered.reshape(by_time), blocks.reshape(by_time))
    time_part = lax.all_to_all(derived.reshape(blocks.shape), "tm", 0, 0, tiled=True)
    parts = add_flux(core, *parts, flux)
    return add_time(*parts, time_part)


def solution(mesh):
    split = P("tm", None, "space", None, None)
    cells = P("space", None, None)
    return jax.shard_map(
        on_device,
        mesh=mesh,
        in_specs=(split, split, cells, cells, cells),
        out_specs=(split, split),
        check_vma=False,
    )
```

```python
import functools

import jax
import jax.numpy as jnp
from jax import lax
from jax.experimental import pallas as pl
from jax.experimental.pallas import tpu as pltpu
from jax.sharding import PartitionSpec as P
import numpy as np

NT = 16
NU_INF = 0.0616
NU_ZERO = 1.0
LAMBDA_SQ = 3.313 * 3.313
POWER = (0.3568 - 1.0) / 2.0
BRINKMAN_MAX = 8.0
RAMP_SHAPE = 0.1
TIME_SCALE = 0.25

PLANES = 4
ROWS = 64
LANES = 128
TOP = 8
PADDED = ROWS + 2 * TOP
TILE = 32
UNROLL = 2
VMEM_LIMIT = 56 << 20
EARLY_COST = 20_000_000_000
LATE_COST = 40_000_000_000
ADD_LIMIT = 12 << 20
GATED = False

MU_A = 0.25 * NU_INF
MU_B = 0.25 * (NU_ZERO - NU_INF)
SHEAR = LAMBDA_SQ / 8.0
DMU = (NU_ZERO - NU_INF) * POWER * LAMBDA_SQ / 16.0


def viscosity(square_sum):
    q = 1.0 + SHEAR * square_sum
    log_q = jnp.log(q)
    return MU_A + MU_B * jnp.exp(POWER * log_q), DMU * jnp.exp((POWER - 1.0) * log_q)


def outer_cell(u, lam, axis):
    strain = [u[j] + u[j] if j == axis else u[j] for j in range(3)]
    rate = [lam[j] + lam[j] if j == axis else lam[j] for j in range(3)]
    others = [j for j in range(3) if j != axis]
    square = sum(strain[j] * strain[j] for j in others)
    cross = sum(strain[j] * rate[j] for j in others)
    square = square + square + strain[axis] * strain[axis]
    cross = cross + cross + strain[axis] * rate[axis]
    mu, dmu = viscosity(square)
    slope = dmu * cross
    return [mu * s for s in strain], [mu * e + slope * s for s, e in zip(strain, rate)]


def stencil_tools(inflow_ref, w, tx, fx, ty, fy, out_f, out_a, density_ref, mask_ref, labels_ref):
    lane = lax.broadcasted_iota(jnp.int32, (TILE, LANES), 1)
    is_first = lane == 0
    is_last = lane == LANES - 1

    def along_z(f):
        up = jnp.where(is_last, 0.0, pltpu.roll(f, LANES - 1, 1))
        down = jnp.where(is_first, 0.0, pltpu.roll(f, 1, 1))
        return up - down

    def along_z_outer(f, outer):
        up = jnp.where(is_last, -outer, pltpu.roll(f, LANES - 1, 1))
        down = jnp.where(is_first, outer, pltpu.roll(f, 1, 1))
        return up - down

    def tile_work(i, p, t, interior):
        r = TOP + pl.multiple_of(t * TILE, 8)
        here = pl.ds(r, TILE)
        u = [w[i, j, p, here, :] for j in range(3)]
        lam = [w[i, 3 + j, p, here, :] for j in range(3)]
        grads, rates = [], []
        for base, values, into in ((0, u, grads), (3, lam, rates)):
            into.append([w[i, base + j, p + 1, here, :] - w[i, base + j, p - 1, here, :] for j in range(3)])
            into.append(
                [w[i, base + j, p, pl.ds(r + 1, TILE), :] - w[i, base + j, p, pl.ds(r - 1, TILE), :] for j in range(3)]
            )
            into.append([along_z(v) for v in values])
        strain = [[grads[k][j] + grads[j][k] for k in range(3)] for j in range(3)]
        rate = [[rates[k][j] + rates[j][k] for k in range(3)] for j in range(3)]
        pairs = ((0, 1), (0, 2), (1, 2))
        square = sum(strain[j][k] * strain[j][k] for j, k in pairs)
        cross = sum(strain[j][k] * rate[j][k] for j, k in pairs)
        square = square + square + sum(strain[j][j] * strain[j][j] for j in range(3))
        cross = cross + cross + sum(strain[j][j] * rate[j][j] for j in range(3))
        mu, dmu = viscosity(square)
        slope = dmu * cross
        half_u = [0.5 * v for v in u]
        half_p = 0.5 * w[i, 6, p, here, :]
        half_q = 0.5 * w[i, 7, p, here, :]

        def flux(j, k):
            t_jk = mu * strain[j][k]
            f_jk = mu * rate[j][k] + slope * strain[j][k] + half_u[k] * lam[j]
            if j == k:
                t_jk, f_jk = t_jk - half_p, f_jk + half_q
            return t_jk, f_jk

        for j in range(3):
            t_jk, f_jk = flux(j, 0)
            tx[i, j, p, pl.ds(r - TOP, TILE), :] = t_jk
            fx[i, j, p, pl.ds(r - TOP, TILE), :] = f_jk
        if not interior:
            return
        q = p - 2
        out_rows = pl.ds(r - TOP, TILE)
        for j in range(3):
            t_jk, f_jk = flux(j, 1)
            ty[j, q, here, :] = t_jk
            fy[j, q, here, :] = f_jk
        outer_t, outer_f = outer_cell(u, lam, 2)
        design = jnp.where(mask_ref[q, out_rows, :] == 1, density_ref[q, out_rows, :], 1.0)
        label = labels_ref[q, out_rows, :]
        ramp = (BRINKMAN_MAX * RAMP_SHAPE) * (1.0 - design) / (RAMP_SHAPE + design)
        penalty = jnp.where(label == 0, ramp, BRINKMAN_MAX)
        target = jnp.where(label == 2, inflow_ref[i], 0.0)
        half_lam = [0.5 * v for v in lam]
        for j in range(3):
            t_jk, f_jk = flux(j, 2)
            shifted = u[j] - target if j == 0 else u[j]
            out_f[i, j, q, out_rows, :] = (
                sum(half_u[k] * grads[k][j] for k in range(3)) - along_z_outer(t_jk, outer_t[j]) + penalty * shifted
            )
            out_a[i, j, q, out_rows, :] = (
                sum(half_lam[k] * grads[j][k] for k in range(3)) - along_z_outer(f_jk, outer_f[j]) + penalty * lam[j]
            )
        out_f[i, 3, q, out_rows, :] = 0.25 * (strain[0][0] + strain[1][1] + strain[2][2])
        out_a[i, 3, q, out_rows, :] = -0.25 * (rate[0][0] + rate[1][1] + rate[2][2])

    def y_edges(i, q):
        p = q + 2
        for first, keep, row, sign in ((TOP, 0, TOP - 1, 1.0), (TOP + ROWS - 8, 7, TOP + ROWS, -1.0)):
            u = [w[i, j, p, first : first + 8, :] for j in range(3)]
            lam = [w[i, 3 + j, p, first : first + 8, :] for j in range(3)]
            outer_t, outer_f = outer_cell(u, lam, 1)
            for j in range(3):
                ty[j, q, row : row + 1, :] = sign * outer_t[j][keep : keep + 1]
                fy[j, q, row : row + 1, :] = sign * outer_f[j][keep : keep + 1]

    def collect(i, p, t, with_x, with_y):
        q = p - 2
        r = pl.multiple_of(t * TILE, 8)
        for out, x_flux, y_flux in ((out_f, tx, ty), (out_a, fx, fy)):
            for j in range(3):
                total = out[i, j, q, pl.ds(r, TILE), :]
                if with_x:
                    total -= x_flux[i, j, p + 1, pl.ds(r, TILE), :] - x_flux[i, j, p - 1, pl.ds(r, TILE), :]
                if with_y:
                    total -= (
                        y_flux[j, q, pl.ds(r + TOP + 1, TILE), :] - y_flux[j, q, pl.ds(r + TOP - 1, TILE), :]
                    )
                out[i, j, q, pl.ds(r, TILE), :] = total

    def over(first, planes, work):
        tiles = ROWS // TILE

        def step(n, _):
            work(first + n // tiles, n % tiles)
            return 0

        lax.fori_loop(0, planes * tiles, step, 0, unroll=UNROLL)

    return tile_work, y_edges, collect, over


def clear_edges(w, i, first, planes):
    zero = jnp.zeros((TOP, LANES), jnp.float32)

    def clear(p, _):
        for c in range(6):
            w[i, c, first + p, 0:TOP, :] = zero
            w[i, c, first + p, TOP + ROWS : PADDED, :] = zero
        return 0

    lax.fori_loop(0, planes, clear, 0)


def early_kernel(
    core_ref, inflow_ref, flow_ref, adj_ref, near_ref, density_hbm, mask_hbm, labels_hbm,
    flow_out, adj_out, tx_out, fx_out,
    out_f, out_a, density_ref, mask_ref, labels_ref, w, tx, fx, ty, fy, sems, cell_sems, out_sems,
):
    insts = out_f.shape[0]
    core = core_ref[0]
    data = pl.ds(TOP, ROWS)
    reads, writes = [], []
    three = pl.ds(1 - core, 3)
    for i in range(insts):
        copies = []
        for source, base, last in ((flow_ref, 0, 6), (adj_ref, 3, 7)):
            copies.append((source.at[i, 0:3], w.at[i, base : base + 3, 2:6, data, :]))
            copies.append((source.at[i, 3], w.at[i, last, 2:6, data, :]))
        for n in range(2):
            for j in range(3):
                copies.append((near_ref.at[i, n, 2 * j : 2 * j + 2], w.at[i, 3 * n + j, pl.ds(6 - 6 * core, 2), data, :]))
            copies.append((near_ref.at[i, n, 6], w.at[i, 6 + n, 6 - 5 * core, data, :]))
        reads.append([pltpu.make_async_copy(a, b, sems.at[i, k]) for k, (a, b) in enumerate(copies)])
        copies = [(a.at[i, :, three], b.at[i, :, three]) for a, b in ((out_f, flow_out), (out_a, adj_out))]
        copies += [(a.at[i, :, 3:5], b.at[i]) for a, b in ((tx, tx_out), (fx, fx_out))]
        writes.append([pltpu.make_async_copy(a, b, out_sems.at[i, k]) for k, (a, b) in enumerate(copies)])
    cells = ((density_hbm, density_ref), (mask_hbm, mask_ref), (labels_hbm, labels_ref))
    reads[0] += [pltpu.make_async_copy(a, b, cell_sems.at[k]) for k, (a, b) in enumerate(cells)]
    for group in reads:
        for h in group:
            h.start()
    for i in range(insts):
        clear_edges(w, i, 0, 8)
    tile_work, y_edges, collect, over = stencil_tools(
        inflow_ref, w, tx, fx, ty, fy, out_f, out_a, density_ref, mask_ref, labels_ref
    )
    for i in range(insts):
        for h in reads[i]:
            h.wait()
        over(6 - 5 * core, 1, lambda p, t: tile_work(i, p, t, False))
        over(3 - core, 3, lambda p, t: tile_work(i, p, t, True))

        def edges(n, _):
            y_edges(i, 1 - core + n)
            return 0

        lax.fori_loop(0, 3, edges, 0)
        over(4 - 2 * core, 2, lambda p, t: collect(i, p, t, True, True))
        over(3 + core, 1, lambda p, t: collect(i, p, t, False, True))
        for h in writes[i]:
            h.start()
    for group in writes:
        for h in group:
            h.wait()


def late_kernel(core_ref, inflow_ref, flow_ref, adj_ref, far_ref, *refs):
    cells_hbm, (_, _, tx_part, fx_part, flow_out, adj_out, sent), refs = refs[:3], refs[3:10], refs[10:]
    out_f, out_a, density_ref, mask_ref, labels_ref, w, tx, fx, ty, fy, sems, part_sems, cell_sems, out_sems = refs
    insts = out_f.shape[0]
    core = core_ref[0]
    at_end = inflow_ref[insts]
    data = pl.ds(TOP, ROWS)
    pair, partial, own = pl.ds(2 * core, 2), pl.ds(1 + core, 1), pl.ds(2 + 2 * core, 2)
    edge, last = 2 + 3 * core, 3 * core
    reads, parts, writes = [], [], []
    for i in range(insts):
        copies = []
        for n, source in enumerate((flow_ref, adj_ref)):
            vel = slice(3 * n, 3 * n + 3)
            copies.append((source.at[i, 0:3, pair], w.at[i, vel, own, data, :]))
            copies.append((source.at[i, 3, pair], w.at[i, 6 + n, own, data, :]))
            copies.append((far_ref.at[i, n], w.at[i, vel, 1 + 5 * core, data, :]))
        reads.append([pltpu.make_async_copy(a, b, sems.at[i, k]) for k, (a, b) in enumerate(copies)])
        copies = [(a.at[i, :, partial], b.at[i, :, partial]) for a, b in ((flow_out, out_f), (adj_out, out_a))]
        copies += [(a.at[i], b.at[i, :, 3:5]) for a, b in ((tx_part, tx), (fx_part, fx))]
        parts.append([pltpu.make_async_copy(a, b, part_sems.at[i, k]) for k, (a, b) in enumerate(copies)])
        copies = [(a.at[i, :, edge], sent.at[i, n]) for n, a in enumerate((tx, fx))]
        copies += [(a.at[i, :, pair], b.at[i, :, pair]) for a, b in ((out_f, flow_out), (out_a, adj_out))]
        writes.append([pltpu.make_async_copy(a, b, out_sems.at[i, k]) for k, (a, b) in enumerate(copies)])
    here = pl.ds(last, 1)
    cells = zip(cells_hbm, (density_ref, mask_ref, labels_ref))
    reads[0] += [pltpu.make_async_copy(a.at[here], b.at[here], cell_sems.at[k]) for k, (a, b) in enumerate(cells)]
    for i in range(insts):
        for h in reads[i] + parts[i]:
            h.start()
    for i in range(insts):
        clear_edges(w, i, 1 + 3 * core, 3)
    tile_work, y_edges, collect, over = stencil_tools(
        inflow_ref, w, tx, fx, ty, fy, out_f, out_a, density_ref, mask_ref, labels_ref
    )
    sign = at_end * (1.0 - 2.0 * core.astype(jnp.float32))

    def beyond(i, t):
        r = pl.multiple_of(t * TILE, 8)
        here = pl.ds(r + TOP, TILE)
        u = [w[i, j, edge, here, :] for j in range(3)]
        lam = [w[i, 3 + j, edge, here, :] for j in range(3)]
        outer_t, outer_f = outer_cell(u, lam, 0)
        for j in range(3):
            tx[i, j, 1 + 5 * core, pl.ds(r, TILE), :] = sign * outer_t[j]
            fx[i, j, 1 + 5 * core, pl.ds(r, TILE), :] = sign * outer_f[j]

    for i in range(insts):
        for h in reads[i]:
            h.wait()
        over(edge, 1, lambda p, t: tile_work(i, p, t, True))
        for h in writes[i][:2]:
            h.start()
        y_edges(i, last)
        over(edge, 1, lambda p, t: beyond(i, t))
        for h in parts[i]:
            h.wait()
        over(edge, 1, lambda p, t: collect(i, p, t, True, True))
        over(3 + core, 1, lambda p, t: collect(i, p, t, True, False))
        for h in writes[i][2:]:
            h.start()
    for group in writes:
        for h in group:
            h.wait()


def load_kernel(f_ref, a_ref, total, sems):
    insts = f_ref.shape[0]
    work = [(i, n) for i in range(insts) for n in range(2)]
    reads = []
    for k, (i, n) in enumerate(work):
        reads.append(pltpu.make_async_copy((f_ref, a_ref)[n].at[i, 0:3], total.at[i, n], sems.at[k]))
        reads[-1].start()
    for read in reads:
        read.wait()


def load_parts(flow_part, adj_part):
    insts = flow_part.shape[0]
    return pl.pallas_call(
        load_kernel,
        out_shape=jax.ShapeDtypeStruct((insts, 2, 3) + flow_part.shape[2:], jnp.float32),
        in_specs=[pl.BlockSpec(memory_space=pltpu.HBM)] * 2,
        out_specs=pl.BlockSpec(memory_space=pltpu.VMEM),
        scratch_shapes=[pltpu.SemaphoreType.DMA((2 * insts,))],
        compiler_params=pltpu.CompilerParams(vmem_limit_bytes=ADD_LIMIT),
        name="load_parts",
    )(flow_part, adj_part)


def flux_kernel(core_ref, part, flux, total):
    core = core_ref[0]
    sign = 1.0 - 2.0 * core.astype(jnp.float32)
    for i in range(part.shape[0]):
        for n in range(2):
            total[i, n] = part[i, n]
            total[i, n, :, 3 * core] = part[i, n, :, 3 * core] + sign * flux[i, n]


def add_flux(core, part, flux):
    whole = pl.BlockSpec(memory_space=pltpu.VMEM)
    return pl.pallas_call(
        flux_kernel,
        out_shape=jax.ShapeDtypeStruct(part.shape, jnp.float32),
        in_specs=[pl.BlockSpec(memory_space=pltpu.SMEM)] + [whole] * 2,
        out_specs=whole,
        compiler_params=pltpu.CompilerParams(vmem_limit_bytes=ADD_LIMIT),
        cost_estimate=pl.CostEstimate(flops=LATE_COST, bytes_accessed=8_000_000, transcendentals=0),
        name="add_flux",
    )(core, part, flux)


def add_kernel(f_ref, a_ref, part, times, out_f, out_a, total, sems):
    insts = out_f.shape[0]
    writes = []
    for i in range(insts):
        for n in range(2):
            for j in range(3):
                for b in range(2 * PLANES):
                    q, rows = block_cells(b)
                    total[i, n, j, q, rows, :] = part[i, n, j, q, rows, :] + times[b, i, 3 * n + j]
                out = (out_f, out_a)[n].at[i, j]
                writes.append(pltpu.make_async_copy(total.at[i, n, j], out, sems.at[len(writes)]))
                writes[-1].start()
    for write in writes:
        write.wait()


def add_time(flow_part, adj_part, part, time_part):
    space = pl.BlockSpec(memory_space=pltpu.HBM)
    insts = flow_part.shape[0]
    shape = jax.ShapeDtypeStruct(flow_part.shape, jnp.float32)
    return pl.pallas_call(
        add_kernel,
        out_shape=(shape, shape),
        in_specs=[space] * 2 + [pl.BlockSpec(memory_space=pltpu.VMEM)] * 2,
        out_specs=[space] * 2,
        scratch_shapes=[pltpu.VMEM(part.shape, jnp.float32), pltpu.SemaphoreType.DMA((6 * insts,))],
        compiler_params=pltpu.CompilerParams(vmem_limit_bytes=ADD_LIMIT),
        input_output_aliases={0: 0, 1: 1},
        name="add_time",
    )(flow_part, adj_part, part, time_part)


def stencil(kernel, name, cost, out_shapes, core, inflow, flow, adj, halos, cells, *parts):
    insts = flow.shape[0]
    space = pl.BlockSpec(memory_space=pltpu.HBM)
    scalar = pl.BlockSpec(memory_space=pltpu.SMEM)
    like = lambda a: pltpu.VMEM(a.shape, a.dtype)
    late = len(parts) > 0
    return pl.pallas_call(
        kernel,
        out_shape=[jax.ShapeDtypeStruct(s, jnp.float32) for s in out_shapes],
        in_specs=[scalar] * 2 + [space] * (2 + len(halos) + len(cells) + len(parts)),
        out_specs=[space] * len(out_shapes),
        scratch_shapes=[like(flow), like(flow)]
        + [like(a) for a in cells]
        + [pltpu.VMEM((insts, 8, 8, PADDED, LANES), jnp.float32)]
        + [pltpu.VMEM((insts, 3, 8, ROWS, LANES), jnp.float32)] * 2
        + [pltpu.VMEM((3, PLANES, PADDED, LANES), jnp.float32)] * 2
        + [pltpu.SemaphoreType.DMA((insts, 12))]
        + ([pltpu.SemaphoreType.DMA((insts, 4))] if late else [])
        + [pltpu.SemaphoreType.DMA((3,)), pltpu.SemaphoreType.DMA((insts, 4))],
        compiler_params=pltpu.CompilerParams(vmem_limit_bytes=VMEM_LIMIT),
        cost_estimate=pl.CostEstimate(flops=cost, bytes_accessed=8_000_000, transcendentals=400_000),
        input_output_aliases={5 + len(halos) + len(cells) - 1 + k: k for k in range(2)} if late else {},
        name=name,
    )(core, inflow, flow, adj, *halos, *cells, *parts)


def spectral_row():
    k = np.arange(1, 8)
    return [float(v) for v in TIME_SCALE * 0.5 * np.where(k % 2 == 0, 1.0, -1.0) / np.tan(np.pi * k / NT)]


def time_kernel(x_ref, sent_hbm, out_hbm, out_ref, sems):
    comps, tiles = x_ref.shape[1], x_ref.shape[2] // 8
    writes = [pltpu.make_async_copy(out_ref.at[:, c], out_hbm.at[:, c], sems.at[c]) for c in range(comps)]
    for c in range(comps):
        coef = [v if c < comps // 2 else -v for v in spectral_row()]

        def step(n, _):
            rows = pl.ds(pl.multiple_of(n * 8, 8), 8)
            x = [x_ref[m, c, rows, :] for m in range(NT)]
            for m in range(NT // 2):
                diff = [x[(m - k) % NT] - x[(m + k) % NT] for k in range(1, 8)]
                out_ref[m, c, rows, :] = sum(coef[k - 1] * diff[k - 1] for k in range(1, 8))
                out_ref[m + 8, c, rows, :] = -sum(coef[k - 1] * diff[7 - k] for k in range(1, 8))
            return 0

        lax.fori_loop(0, tiles, step, 0, unroll=4)
        writes[c].start()
    for h in writes:
        h.wait()


def time_derivative(x, sent):
    return pl.pallas_call(
        time_kernel,
        out_shape=jax.ShapeDtypeStruct(x.shape, jnp.float32),
        in_specs=[pl.BlockSpec(memory_space=pltpu.VMEM), pl.BlockSpec(memory_space=pltpu.HBM)],
        out_specs=pl.BlockSpec(memory_space=pltpu.HBM),
        scratch_shapes=[pltpu.VMEM(x.shape, jnp.float32), pltpu.SemaphoreType.DMA((x.shape[1],))],
        compiler_params=pltpu.CompilerParams(vmem_limit_bytes=8 << 20),
        cost_estimate=pl.CostEstimate(flops=12_000_000, bytes_accessed=3_200_000, transcendentals=0),
        input_output_aliases={1: 0},
        name="time_derivative",
    )(x, sent)


def block_cells(b):
    half = ROWS // 2
    return b // 2, slice(b % 2 * half, (b % 2 + 1) * half)


def halo_copies(state_ref, ref, first, near):
    copies = [(state_ref.at[:, j, pl.ds(first, 2)], ref.at[:, 2 * j : 2 * j + 2]) for j in range(3)]
    return copies + [(state_ref.at[:, 3, pl.ds(near, 1)], ref.at[:, 6:7])]


def block_copies(flow_ref, adj_ref, ref, b):
    q, rows = block_cells(b)
    return [(flow_ref.at[:, 0:3, q, rows], ref.at[b, :, 0:3]), (adj_ref.at[:, 0:3, q, rows], ref.at[b, :, 3:6])]


def through_vmem(groups, sems):
    flat = [c for copies, _ in groups for c in copies] + [write for _, write in groups]
    handles = [pltpu.make_async_copy(a, b, sems.at[i]) for i, (a, b) in enumerate(flat)]
    writes = handles[len(handles) - len(groups) :]
    for h in handles[: len(handles) - len(groups)]:
        h.start()
    done = 0
    for (copies, _), write in zip(groups, writes):
        for h in handles[done : done + len(copies)]:
            h.wait()
        done += len(copies)
        write.start()
    for write in writes:
        write.wait()


def pack_kernel(core_ref, flow_ref, adj_ref, blocks_ref, near_ref, far_ref, blocks, near, far, sems):
    core = core_ref[0]
    states = (flow_ref, adj_ref)
    copies = sum([halo_copies(state, near.at[:, n], 2 - 2 * core, 3 - 3 * core) for n, state in enumerate(states)], [])
    halos = [(copies, (near, near_ref))]
    copies = [(state.at[:, 0:3, 3 * core], far.at[:, n]) for n, state in enumerate(states)]
    halos.append((copies, (far, far_ref)))
    groups = []
    for b in range(2 * PLANES):
        groups.append((block_copies(flow_ref, adj_ref, blocks, b), (blocks.at[b], blocks_ref.at[b])))
    through_vmem(halos + groups, sems)


def pack(core, flow, adj):
    insts = flow.shape[0]
    space = pl.BlockSpec(memory_space=pltpu.HBM)
    halo = (insts, 2, 7, ROWS, LANES)
    blocks = (2 * PLANES, insts, 6, ROWS // 2, LANES)
    shapes = [blocks, halo, (insts, 2, 3, ROWS, LANES)]
    copies = 8 + 1 + 2 + 1 + 6 * PLANES
    return pl.pallas_call(
        pack_kernel,
        out_shape=[jax.ShapeDtypeStruct(s, jnp.float32) for s in shapes],
        in_specs=[pl.BlockSpec(memory_space=pltpu.SMEM)] + [space] * 2,
        out_specs=[space] * len(shapes),
        scratch_shapes=[
            pltpu.VMEM(blocks, jnp.float32),
            pltpu.VMEM(halo, jnp.float32),
            pltpu.VMEM(shapes[2], jnp.float32),
            pltpu.SemaphoreType.DMA((copies,)),
        ],
        compiler_params=pltpu.CompilerParams(vmem_limit_bytes=VMEM_LIMIT),
        name="pack",
    )(core, flow, adj)


def on_device(flow, adj, density, mask, labels):
    insts = flow.shape[0]
    count = lax.axis_size("space")
    instances = lax.axis_index("tm") * insts + jnp.arange(insts, dtype=jnp.int32)
    inflow = 1.0 + 0.5 * jnp.sin(2.0 * jnp.pi * instances.astype(jnp.float32) / NT)

    core = lax.axis_index("space") % 2
    at_end = (lax.axis_index("space") == 0) | (lax.axis_index("space") == count - 1)
    core = core.reshape(1)
    scalars = jnp.append(inflow, at_end.astype(jnp.float32))
    blocks, near, far = pack(core, flow, adj)
    near = lax.ppermute(near, "space", [p for i in range(0, count, 2) for p in ((i, i + 1), (i + 1, i))])
    across = [p for i in range(1, count - 1, 2) for p in ((i, i + 1), (i + 1, i))]
    far = lax.ppermute(far, "space", across)
    if GATED:
        blocks, near = lax.optimization_barrier((blocks, near))
    gathered = lax.all_to_all(blocks, "tm", 0, 0, tiled=True)
    cells = (density, mask, labels)
    edge = (insts, 3, 2, ROWS, LANES)
    parts = stencil(
        early_kernel, "early", EARLY_COST, [flow.shape] * 2 + [edge] * 2, core, scalars, flow, adj, [near], cells
    )
    shapes = [flow.shape] * 2 + [(insts, 2, 3, ROWS, LANES)]
    *parts, flux = stencil(late_kernel, "late", LATE_COST, shapes, core, scalars, flow, adj, [far], cells, *parts)
    flux = lax.ppermute(flux, "space", across)
    gathered, *parts = lax.optimization_barrier((gathered, *parts))
    by_time = (NT,) + blocks.shape[2:]
    derived = time_derivative(gathered.reshape(by_time), blocks.reshape(by_time))
    time_part = lax.all_to_all(derived.reshape(blocks.shape), "tm", 0, 0, tiled=True)
    return add_time(*parts, add_flux(core, load_parts(*parts), flux), time_part)


def solution(mesh):
    split = P("tm", None, "space", None, None)
    cells = P("space", None, None)
    return jax.shard_map(
        on_device,
        mesh=mesh,
        in_specs=(split, split, cells, cells, cells),
        out_specs=(split, split),
        check_vma=False,
    )
```

```python
import functools

import jax
import jax.numpy as jnp
from jax import lax
from jax.experimental import pallas as pl
from jax.experimental.pallas import tpu as pltpu
from jax.sharding import PartitionSpec as P
import numpy as np

NT = 16
NU_INF = 0.0616
NU_ZERO = 1.0
LAMBDA_SQ = 3.313 * 3.313
POWER = (0.3568 - 1.0) / 2.0
BRINKMAN_MAX = 8.0
RAMP_SHAPE = 0.1
TIME_SCALE = 0.25

PLANES = 4
ROWS = 64
LANES = 128
TOP = 8
PADDED = ROWS + 2 * TOP
TILE = 32
UNROLL = 2
VMEM_LIMIT = 56 << 20
EARLY_COST = 20_000_000_000
LATE_COST = 40_000_000_000
ADD_LIMIT = 12 << 20
GATED = False

MU_A = 0.25 * NU_INF
MU_B = 0.25 * (NU_ZERO - NU_INF)
SHEAR = LAMBDA_SQ / 8.0
DMU = (NU_ZERO - NU_INF) * POWER * LAMBDA_SQ / 16.0


def viscosity(square_sum):
    q = 1.0 + SHEAR * square_sum
    log_q = jnp.log(q)
    return MU_A + MU_B * jnp.exp(POWER * log_q), DMU * jnp.exp((POWER - 1.0) * log_q)


def outer_cell(u, lam, axis):
    strain = [u[j] + u[j] if j == axis else u[j] for j in range(3)]
    rate = [lam[j] + lam[j] if j == axis else lam[j] for j in range(3)]
    others = [j for j in range(3) if j != axis]
    square = sum(strain[j] * strain[j] for j in others)
    cross = sum(strain[j] * rate[j] for j in others)
    square = square + square + strain[axis] * strain[axis]
    cross = cross + cross + strain[axis] * rate[axis]
    mu, dmu = viscosity(square)
    slope = dmu * cross
    return [mu * s for s in strain], [mu * e + slope * s for s, e in zip(strain, rate)]


def stencil_tools(inflow_ref, w, tx, fx, ty, fy, out_f, out_a, density_ref, mask_ref, labels_ref):
    lane = lax.broadcasted_iota(jnp.int32, (TILE, LANES), 1)
    is_first = lane == 0
    is_last = lane == LANES - 1

    def along_z(f):
        up = jnp.where(is_last, 0.0, pltpu.roll(f, LANES - 1, 1))
        down = jnp.where(is_first, 0.0, pltpu.roll(f, 1, 1))
        return up - down

    def along_z_outer(f, outer):
        up = jnp.where(is_last, -outer, pltpu.roll(f, LANES - 1, 1))
        down = jnp.where(is_first, outer, pltpu.roll(f, 1, 1))
        return up - down

    def tile_work(i, p, t, interior):
        r = TOP + pl.multiple_of(t * TILE, 8)
        here = pl.ds(r, TILE)
        u = [w[i, j, p, here, :] for j in range(3)]
        lam = [w[i, 3 + j, p, here, :] for j in range(3)]
        grads, rates = [], []
        for base, values, into in ((0, u, grads), (3, lam, rates)):
            into.append([w[i, base + j, p + 1, here, :] - w[i, base + j, p - 1, here, :] for j in range(3)])
            into.append(
                [w[i, base + j, p, pl.ds(r + 1, TILE), :] - w[i, base + j, p, pl.ds(r - 1, TILE), :] for j in range(3)]
            )
            into.append([along_z(v) for v in values])
        strain = [[grads[k][j] + grads[j][k] for k in range(3)] for j in range(3)]
        rate = [[rates[k][j] + rates[j][k] for k in range(3)] for j in range(3)]
        pairs = ((0, 1), (0, 2), (1, 2))
        square = sum(strain[j][k] * strain[j][k] for j, k in pairs)
        cross = sum(strain[j][k] * rate[j][k] for j, k in pairs)
        square = square + square + sum(strain[j][j] * strain[j][j] for j in range(3))
        cross = cross + cross + sum(strain[j][j] * rate[j][j] for j in range(3))
        mu, dmu = viscosity(square)
        slope = dmu * cross
        half_u = [0.5 * v for v in u]
        half_p = 0.5 * w[i, 6, p, here, :]
        half_q = 0.5 * w[i, 7, p, here, :]

        def flux(j, k):
            t_jk = mu * strain[j][k]
            f_jk = mu * rate[j][k] + slope * strain[j][k] + half_u[k] * lam[j]
            if j == k:
                t_jk, f_jk = t_jk - half_p, f_jk + half_q
            return t_jk, f_jk

        for j in range(3):
            t_jk, f_jk = flux(j, 0)
            tx[i, j, p, pl.ds(r - TOP, TILE), :] = t_jk
            fx[i, j, p, pl.ds(r - TOP, TILE), :] = f_jk
        if not interior:
            return
        q = p - 2
        out_rows = pl.ds(r - TOP, TILE)
        for j in range(3):
            t_jk, f_jk = flux(j, 1)
            ty[j, q, here, :] = t_jk
            fy[j, q, here, :] = f_jk
        outer_t, outer_f = outer_cell(u, lam, 2)
        design = jnp.where(mask_ref[q, out_rows, :] == 1, density_ref[q, out_rows, :], 1.0)
        label = labels_ref[q, out_rows, :]
        ramp = (BRINKMAN_MAX * RAMP_SHAPE) * (1.0 - design) / (RAMP_SHAPE + design)
        penalty = jnp.where(label == 0, ramp, BRINKMAN_MAX)
        target = jnp.where(label == 2, inflow_ref[i], 0.0)
        half_lam = [0.5 * v for v in lam]
        for j in range(3):
            t_jk, f_jk = flux(j, 2)
            shifted = u[j] - target if j == 0 else u[j]
            out_f[i, j, q, out_rows, :] = (
                sum(half_u[k] * grads[k][j] for k in range(3)) - along_z_outer(t_jk, outer_t[j]) + penalty * shifted
            )
            out_a[i, j, q, out_rows, :] = (
                sum(half_lam[k] * grads[j][k] for k in range(3)) - along_z_outer(f_jk, outer_f[j]) + penalty * lam[j]
            )
        out_f[i, 3, q, out_rows, :] = 0.25 * (strain[0][0] + strain[1][1] + strain[2][2])
        out_a[i, 3, q, out_rows, :] = -0.25 * (rate[0][0] + rate[1][1] + rate[2][2])

    def y_edges(i, q):
        p = q + 2
        for first, keep, row, sign in ((TOP, 0, TOP - 1, 1.0), (TOP + ROWS - 8, 7, TOP + ROWS, -1.0)):
            u = [w[i, j, p, first : first + 8, :] for j in range(3)]
            lam = [w[i, 3 + j, p, first : first + 8, :] for j in range(3)]
            outer_t, outer_f = outer_cell(u, lam, 1)
            for j in range(3):
                ty[j, q, row : row + 1, :] = sign * outer_t[j][keep : keep + 1]
                fy[j, q, row : row + 1, :] = sign * outer_f[j][keep : keep + 1]

    def collect(i, p, t, with_x, with_y):
        q = p - 2
        r = pl.multiple_of(t * TILE, 8)
        for out, x_flux, y_flux in ((out_f, tx, ty), (out_a, fx, fy)):
            for j in range(3):
                total = out[i, j, q, pl.ds(r, TILE), :]
                if with_x:
                    total -= x_flux[i, j, p + 1, pl.ds(r, TILE), :] - x_flux[i, j, p - 1, pl.ds(r, TILE), :]
                if with_y:
                    total -= (
                        y_flux[j, q, pl.ds(r + TOP + 1, TILE), :] - y_flux[j, q, pl.ds(r + TOP - 1, TILE), :]
                    )
                out[i, j, q, pl.ds(r, TILE), :] = total

    def over(first, planes, work):
        tiles = ROWS // TILE

        def step(n, _):
            work(first + n // tiles, n % tiles)
            return 0

        lax.fori_loop(0, planes * tiles, step, 0, unroll=UNROLL)

    return tile_work, y_edges, collect, over


def clear_edges(w, i, first, planes):
    zero = jnp.zeros((TOP, LANES), jnp.float32)

    def clear(p, _):
        for c in range(6):
            w[i, c, first + p, 0:TOP, :] = zero
            w[i, c, first + p, TOP + ROWS : PADDED, :] = zero
        return 0

    lax.fori_loop(0, planes, clear, 0)


def early_kernel(
    core_ref, inflow_ref, flow_ref, adj_ref, near_ref, density_hbm, mask_hbm, labels_hbm,
    flow_out, adj_out, tx_out, fx_out,
    out_f, out_a, density_ref, mask_ref, labels_ref, w, tx, fx, ty, fy, sems, cell_sems, out_sems,
):
    insts = out_f.shape[0]
    core = core_ref[0]
    data = pl.ds(TOP, ROWS)
    reads, writes = [], []
    three = pl.ds(1 - core, 3)
    for i in range(insts):
        copies = []
        for source, base, last in ((flow_ref, 0, 6), (adj_ref, 3, 7)):
            copies.append((source.at[i, 0:3], w.at[i, base : base + 3, 2:6, data, :]))
            copies.append((source.at[i, 3], w.at[i, last, 2:6, data, :]))
        for n in range(2):
            for j in range(3):
                copies.append((near_ref.at[i, n, 2 * j : 2 * j + 2], w.at[i, 3 * n + j, pl.ds(6 - 6 * core, 2), data, :]))
            copies.append((near_ref.at[i, n, 6], w.at[i, 6 + n, 6 - 5 * core, data, :]))
        reads.append([pltpu.make_async_copy(a, b, sems.at[i, k]) for k, (a, b) in enumerate(copies)])
        copies = [(a.at[i, :, three], b.at[i, :, three]) for a, b in ((out_f, flow_out), (out_a, adj_out))]
        copies += [(a.at[i, :, 3:5], b.at[i]) for a, b in ((tx, tx_out), (fx, fx_out))]
        writes.append([pltpu.make_async_copy(a, b, out_sems.at[i, k]) for k, (a, b) in enumerate(copies)])
    cells = ((density_hbm, density_ref), (mask_hbm, mask_ref), (labels_hbm, labels_ref))
    reads[0] += [pltpu.make_async_copy(a, b, cell_sems.at[k]) for k, (a, b) in enumerate(cells)]
    for group in reads:
        for h in group:
            h.start()
    for i in range(insts):
        clear_edges(w, i, 0, 8)
    tile_work, y_edges, collect, over = stencil_tools(
        inflow_ref, w, tx, fx, ty, fy, out_f, out_a, density_ref, mask_ref, labels_ref
    )
    for i in range(insts):
        for h in reads[i]:
            h.wait()
        over(6 - 5 * core, 1, lambda p, t: tile_work(i, p, t, False))
        over(3 - core, 3, lambda p, t: tile_work(i, p, t, True))

        def edges(n, _):
            y_edges(i, 1 - core + n)
            return 0

        lax.fori_loop(0, 3, edges, 0)
        over(4 - 2 * core, 2, lambda p, t: collect(i, p, t, True, True))
        over(3 + core, 1, lambda p, t: collect(i, p, t, False, True))
        for h in writes[i]:
            h.start()
    for group in writes:
        for h in group:
            h.wait()


def late_kernel(core_ref, inflow_ref, flow_ref, adj_ref, far_ref, *refs):
    cells_hbm, (_, _, tx_part, fx_part, flow_out, adj_out, sent), refs = refs[:3], refs[3:10], refs[10:]
    out_f, out_a, density_ref, mask_ref, labels_ref, w, tx, fx, ty, fy, sems, part_sems, cell_sems, out_sems = refs
    insts = out_f.shape[0]
    core = core_ref[0]
    at_end = inflow_ref[insts]
    data = pl.ds(TOP, ROWS)
    pair, partial, own = pl.ds(2 * core, 2), pl.ds(1 + core, 1), pl.ds(2 + 2 * core, 2)
    edge, last = 2 + 3 * core, 3 * core
    reads, writes = [], []
    for i in range(insts):
        copies = []
        for n, source in enumerate((flow_ref, adj_ref)):
            vel = slice(3 * n, 3 * n + 3)
            copies.append((source.at[i, 0:3, pair], w.at[i, vel, own, data, :]))
            copies.append((source.at[i, 3, pair], w.at[i, 6 + n, own, data, :]))
            copies.append((far_ref.at[i, n], w.at[i, vel, 1 + 5 * core, data, :]))
        reads.append([pltpu.make_async_copy(a, b, sems.at[i, k]) for k, (a, b) in enumerate(copies)])
        copies = [(a.at[i, :, edge], sent.at[i, n]) for n, a in enumerate((tx, fx))]
        copies += [(a.at[i, :, last], b.at[i, :, last]) for a, b in ((out_f, flow_out), (out_a, adj_out))]
        writes.append([pltpu.make_async_copy(a, b, out_sems.at[i, k]) for k, (a, b) in enumerate(copies)])
    here = pl.ds(last, 1)
    cells = zip(cells_hbm, (density_ref, mask_ref, labels_ref))
    reads[0] += [pltpu.make_async_copy(a.at[here], b.at[here], cell_sems.at[k]) for k, (a, b) in enumerate(cells)]
    for i in range(insts):
        for h in reads[i]:
            h.start()
    for i in range(insts):
        clear_edges(w, i, 1 + 3 * core, 3)
    tile_work, y_edges, collect, over = stencil_tools(
        inflow_ref, w, tx, fx, ty, fy, out_f, out_a, density_ref, mask_ref, labels_ref
    )

    def beyond(i, t):
        r = pl.multiple_of(t * TILE, 8)
        here = pl.ds(r + TOP, TILE)
        u = [w[i, j, edge, here, :] for j in range(3)]
        lam = [w[i, 3 + j, edge, here, :] for j in range(3)]
        outer_t, outer_f = outer_cell(u, lam, 0)
        for j in range(3):
            out_f[i, j, last, pl.ds(r, TILE), :] += at_end * outer_t[j]
            out_a[i, j, last, pl.ds(r, TILE), :] += at_end * outer_f[j]

    for i in range(insts):
        for h in reads[i]:
            h.wait()
        over(edge, 1, lambda p, t: tile_work(i, p, t, True))
        for h in writes[i][:2]:
            h.start()
        y_edges(i, last)
        over(edge, 1, lambda p, t: beyond(i, t))
        over(edge, 1, lambda p, t: collect(i, p, t, False, True))
        for h in writes[i][2:]:
            h.start()
    for group in writes:
        for h in group:
            h.wait()


def load_kernel(f_ref, a_ref, total, sems):
    insts = f_ref.shape[0]
    work = [(i, n) for i in range(insts) for n in range(2)]
    reads = []
    for k, (i, n) in enumerate(work):
        reads.append(pltpu.make_async_copy((f_ref, a_ref)[n].at[i, 0:3], total.at[i, n], sems.at[k]))
        reads[-1].start()
    for read in reads:
        read.wait()


def load_parts(flow_part, adj_part):
    insts = flow_part.shape[0]
    return pl.pallas_call(
        load_kernel,
        out_shape=jax.ShapeDtypeStruct((insts, 2, 3) + flow_part.shape[2:], jnp.float32),
        in_specs=[pl.BlockSpec(memory_space=pltpu.HBM)] * 2,
        out_specs=pl.BlockSpec(memory_space=pltpu.VMEM),
        scratch_shapes=[pltpu.SemaphoreType.DMA((2 * insts,))],
        compiler_params=pltpu.CompilerParams(vmem_limit_bytes=ADD_LIMIT),
        name="load_parts",
    )(flow_part, adj_part)


def flux_kernel(core_ref, part, flux, leaving, tx_part, fx_part, total):
    core = core_ref[0]
    sign = 1.0 - 2.0 * core.astype(jnp.float32)
    for i in range(part.shape[0]):
        for n in range(2):
            total[i, n] = part[i, n]
            flux_x = (tx_part, fx_part)[n]
            near, next_one = flux_x[i, :, core], flux_x[i, :, 1 - core]
            total[i, n, :, 3 * core] = part[i, n, :, 3 * core] - sign * (near - flux[i, n])
            total[i, n, :, 1 + core] = part[i, n, :, 1 + core] - sign * (next_one - leaving[i, n])


def add_flux(core, part, *fluxes):
    whole = pl.BlockSpec(memory_space=pltpu.VMEM)
    return pl.pallas_call(
        flux_kernel,
        out_shape=jax.ShapeDtypeStruct(part.shape, jnp.float32),
        in_specs=[pl.BlockSpec(memory_space=pltpu.SMEM)] + [whole] * (1 + len(fluxes)),
        out_specs=whole,
        compiler_params=pltpu.CompilerParams(vmem_limit_bytes=ADD_LIMIT),
        cost_estimate=pl.CostEstimate(flops=LATE_COST, bytes_accessed=8_000_000, transcendentals=0),
        name="add_flux",
    )(core, part, *fluxes)


def add_kernel(f_ref, a_ref, part, times, out_f, out_a, total, sems):
    insts = out_f.shape[0]
    writes = []
    for i in range(insts):
        for n in range(2):
            for j in range(3):
                for b in range(2 * PLANES):
                    q, rows = block_cells(b)
                    total[i, n, j, q, rows, :] = part[i, n, j, q, rows, :] + times[b, i, 3 * n + j]
                out = (out_f, out_a)[n].at[i, j]
                writes.append(pltpu.make_async_copy(total.at[i, n, j], out, sems.at[len(writes)]))
                writes[-1].start()
    for write in writes:
        write.wait()


def add_time(flow_part, adj_part, part, time_part):
    space = pl.BlockSpec(memory_space=pltpu.HBM)
    insts = flow_part.shape[0]
    shape = jax.ShapeDtypeStruct(flow_part.shape, jnp.float32)
    return pl.pallas_call(
        add_kernel,
        out_shape=(shape, shape),
        in_specs=[space] * 2 + [pl.BlockSpec(memory_space=pltpu.VMEM)] * 2,
        out_specs=[space] * 2,
        scratch_shapes=[pltpu.VMEM(part.shape, jnp.float32), pltpu.SemaphoreType.DMA((6 * insts,))],
        compiler_params=pltpu.CompilerParams(vmem_limit_bytes=ADD_LIMIT),
        input_output_aliases={0: 0, 1: 1},
        name="add_time",
    )(flow_part, adj_part, part, time_part)


def stencil(kernel, name, cost, out_shapes, core, inflow, flow, adj, halos, cells, *parts):
    insts = flow.shape[0]
    space = pl.BlockSpec(memory_space=pltpu.HBM)
    scalar = pl.BlockSpec(memory_space=pltpu.SMEM)
    like = lambda a: pltpu.VMEM(a.shape, a.dtype)
    late = len(parts) > 0
    return pl.pallas_call(
        kernel,
        out_shape=[jax.ShapeDtypeStruct(s, jnp.float32) for s in out_shapes],
        in_specs=[scalar] * 2 + [space] * (2 + len(halos) + len(cells) + len(parts)),
        out_specs=[space] * len(out_shapes),
        scratch_shapes=[like(flow), like(flow)]
        + [like(a) for a in cells]
        + [pltpu.VMEM((insts, 8, 8, PADDED, LANES), jnp.float32)]
        + [pltpu.VMEM((insts, 3, 8, ROWS, LANES), jnp.float32)] * 2
        + [pltpu.VMEM((3, PLANES, PADDED, LANES), jnp.float32)] * 2
        + [pltpu.SemaphoreType.DMA((insts, 12))]
        + ([pltpu.SemaphoreType.DMA((insts, 4))] if late else [])
        + [pltpu.SemaphoreType.DMA((3,)), pltpu.SemaphoreType.DMA((insts, 4))],
        compiler_params=pltpu.CompilerParams(vmem_limit_bytes=VMEM_LIMIT),
        cost_estimate=pl.CostEstimate(flops=cost, bytes_accessed=8_000_000, transcendentals=400_000),
        input_output_aliases={5 + len(halos) + len(cells) - 1 + k: k for k in range(2)} if late else {},
        name=name,
    )(core, inflow, flow, adj, *halos, *cells, *parts)


def spectral_row():
    k = np.arange(1, 8)
    return [float(v) for v in TIME_SCALE * 0.5 * np.where(k % 2 == 0, 1.0, -1.0) / np.tan(np.pi * k / NT)]


def time_kernel(x_ref, sent_hbm, out_hbm, out_ref, sems):
    comps, tiles = x_ref.shape[1], x_ref.shape[2] // 8
    writes = [pltpu.make_async_copy(out_ref.at[:, c], out_hbm.at[:, c], sems.at[c]) for c in range(comps)]
    for c in range(comps):
        coef = [v if c < comps // 2 else -v for v in spectral_row()]

        def step(n, _):
            rows = pl.ds(pl.multiple_of(n * 8, 8), 8)
            x = [x_ref[m, c, rows, :] for m in range(NT)]
            for m in range(NT // 2):
                diff = [x[(m - k) % NT] - x[(m + k) % NT] for k in range(1, 8)]
                out_ref[m, c, rows, :] = sum(coef[k - 1] * diff[k - 1] for k in range(1, 8))
                out_ref[m + 8, c, rows, :] = -sum(coef[k - 1] * diff[7 - k] for k in range(1, 8))
            return 0

        lax.fori_loop(0, tiles, step, 0, unroll=4)
        writes[c].start()
    for h in writes:
        h.wait()


def time_derivative(x, sent):
    return pl.pallas_call(
        time_kernel,
        out_shape=jax.ShapeDtypeStruct(x.shape, jnp.float32),
        in_specs=[pl.BlockSpec(memory_space=pltpu.VMEM), pl.BlockSpec(memory_space=pltpu.HBM)],
        out_specs=pl.BlockSpec(memory_space=pltpu.HBM),
        scratch_shapes=[pltpu.VMEM(x.shape, jnp.float32), pltpu.SemaphoreType.DMA((x.shape[1],))],
        compiler_params=pltpu.CompilerParams(vmem_limit_bytes=8 << 20),
        cost_estimate=pl.CostEstimate(flops=12_000_000, bytes_accessed=3_200_000, transcendentals=0),
        input_output_aliases={1: 0},
        name="time_derivative",
    )(x, sent)


def block_cells(b):
    half = ROWS // 2
    return b // 2, slice(b % 2 * half, (b % 2 + 1) * half)


def halo_copies(state_ref, ref, first, near):
    copies = [(state_ref.at[:, j, pl.ds(first, 2)], ref.at[:, 2 * j : 2 * j + 2]) for j in range(3)]
    return copies + [(state_ref.at[:, 3, pl.ds(near, 1)], ref.at[:, 6:7])]


def block_copies(flow_ref, adj_ref, ref, b):
    q, rows = block_cells(b)
    return [(flow_ref.at[:, 0:3, q, rows], ref.at[b, :, 0:3]), (adj_ref.at[:, 0:3, q, rows], ref.at[b, :, 3:6])]


def through_vmem(groups, sems):
    flat = [c for copies, _ in groups for c in copies] + [write for _, write in groups]
    handles = [pltpu.make_async_copy(a, b, sems.at[i]) for i, (a, b) in enumerate(flat)]
    writes = handles[len(handles) - len(groups) :]
    for h in handles[: len(handles) - len(groups)]:
        h.start()
    done = 0
    for (copies, _), write in zip(groups, writes):
        for h in handles[done : done + len(copies)]:
            h.wait()
        done += len(copies)
        write.start()
    for write in writes:
        write.wait()


def pack_kernel(core_ref, flow_ref, adj_ref, blocks_ref, near_ref, far_ref, blocks, near, far, sems):
    core = core_ref[0]
    states = (flow_ref, adj_ref)
    copies = sum([halo_copies(state, near.at[:, n], 2 - 2 * core, 3 - 3 * core) for n, state in enumerate(states)], [])
    halos = [(copies, (near, near_ref))]
    copies = [(state.at[:, 0:3, 3 * core], far.at[:, n]) for n, state in enumerate(states)]
    halos.append((copies, (far, far_ref)))
    groups = []
    for b in range(2 * PLANES):
        groups.append((block_copies(flow_ref, adj_ref, blocks, b), (blocks.at[b], blocks_ref.at[b])))
    through_vmem(halos + groups, sems)


def pack(core, flow, adj):
    insts = flow.shape[0]
    space = pl.BlockSpec(memory_space=pltpu.HBM)
    halo = (insts, 2, 7, ROWS, LANES)
    blocks = (2 * PLANES, insts, 6, ROWS // 2, LANES)
    shapes = [blocks, halo, (insts, 2, 3, ROWS, LANES)]
    copies = 8 + 1 + 2 + 1 + 6 * PLANES
    return pl.pallas_call(
        pack_kernel,
        out_shape=[jax.ShapeDtypeStruct(s, jnp.float32) for s in shapes],
        in_specs=[pl.BlockSpec(memory_space=pltpu.SMEM)] + [space] * 2,
        out_specs=[space] * len(shapes),
        scratch_shapes=[
            pltpu.VMEM(blocks, jnp.float32),
            pltpu.VMEM(halo, jnp.float32),
            pltpu.VMEM(shapes[2], jnp.float32),
            pltpu.SemaphoreType.DMA((copies,)),
        ],
        compiler_params=pltpu.CompilerParams(vmem_limit_bytes=VMEM_LIMIT),
        name="pack",
    )(core, flow, adj)


def on_device(flow, adj, density, mask, labels):
    insts = flow.shape[0]
    count = lax.axis_size("space")
    instances = lax.axis_index("tm") * insts + jnp.arange(insts, dtype=jnp.int32)
    inflow = 1.0 + 0.5 * jnp.sin(2.0 * jnp.pi * instances.astype(jnp.float32) / NT)

    core = lax.axis_index("space") % 2
    at_end = (lax.axis_index("space") == 0) | (lax.axis_index("space") == count - 1)
    core = core.reshape(1)
    scalars = jnp.append(inflow, at_end.astype(jnp.float32))
    blocks, near, far = pack(core, flow, adj)
    near = lax.ppermute(near, "space", [p for i in range(0, count, 2) for p in ((i, i + 1), (i + 1, i))])
    across = [p for i in range(1, count - 1, 2) for p in ((i, i + 1), (i + 1, i))]
    far = lax.ppermute(far, "space", across)
    if GATED:
        blocks, near = lax.optimization_barrier((blocks, near))
    gathered = lax.all_to_all(blocks, "tm", 0, 0, tiled=True)
    cells = (density, mask, labels)
    edge = (insts, 3, 2, ROWS, LANES)
    parts = stencil(
        early_kernel, "early", EARLY_COST, [flow.shape] * 2 + [edge] * 2, core, scalars, flow, adj, [near], cells
    )
    shapes = [flow.shape] * 2 + [(insts, 2, 3, ROWS, LANES)]
    edges = parts[2:]
    *parts, leaving = stencil(late_kernel, "late", LATE_COST, shapes, core, scalars, flow, adj, [far], cells, *parts)
    flux = lax.ppermute(leaving, "space", across)
    gathered, *parts = lax.optimization_barrier((gathered, *parts))
    by_time = (NT,) + blocks.shape[2:]
    derived = time_derivative(gathered.reshape(by_time), blocks.reshape(by_time))
    time_part = lax.all_to_all(derived.reshape(blocks.shape), "tm", 0, 0, tiled=True)
    return add_time(*parts, add_flux(core, load_parts(*parts), flux, leaving, *edges), time_part)


def solution(mesh):
    split = P("tm", None, "space", None, None)
    cells = P("space", None, None)
    return jax.shard_map(
        on_device,
        mesh=mesh,
        in_specs=(split, split, cells, cells, cells),
        out_specs=(split, split),
        check_vma=False,
    )
```

```python
import functools

import jax
import jax.numpy as jnp
from jax import lax
from jax.experimental import pallas as pl
from jax.experimental.pallas import tpu as pltpu
from jax.sharding import PartitionSpec as P
import numpy as np

NT = 16
NU_INF = 0.0616
NU_ZERO = 1.0
LAMBDA_SQ = 3.313 * 3.313
POWER = (0.3568 - 1.0) / 2.0
BRINKMAN_MAX = 8.0
RAMP_SHAPE = 0.1
TIME_SCALE = 0.25

PLANES = 4
ROWS = 64
LANES = 128
TOP = 8
PADDED = ROWS + 2 * TOP
TILE = 64
UNROLL = 1
VMEM_LIMIT = 56 << 20
EARLY_COST = 20_000_000_000
LATE_COST = 40_000_000_000
ADD_LIMIT = 12 << 20
GATED = False

MU_A = 0.25 * NU_INF
MU_B = 0.25 * (NU_ZERO - NU_INF)
SHEAR = LAMBDA_SQ / 8.0
DMU = (NU_ZERO - NU_INF) * POWER * LAMBDA_SQ / 16.0


def viscosity(square_sum):
    q = 1.0 + SHEAR * square_sum
    log_q = jnp.log(q)
    return MU_A + MU_B * jnp.exp(POWER * log_q), DMU * jnp.exp((POWER - 1.0) * log_q)


def outer_cell(u, lam, axis):
    strain = [u[j] + u[j] if j == axis else u[j] for j in range(3)]
    rate = [lam[j] + lam[j] if j == axis else lam[j] for j in range(3)]
    others = [j for j in range(3) if j != axis]
    square = sum(strain[j] * strain[j] for j in others)
    cross = sum(strain[j] * rate[j] for j in others)
    square = square + square + strain[axis] * strain[axis]
    cross = cross + cross + strain[axis] * rate[axis]
    mu, dmu = viscosity(square)
    slope = dmu * cross
    return [mu * s for s in strain], [mu * e + slope * s for s, e in zip(strain, rate)]


def stencil_tools(inflow_ref, w, tx, fx, ty, fy, out_f, out_a, density_ref, mask_ref, labels_ref):
    lane = lax.broadcasted_iota(jnp.int32, (TILE, LANES), 1)
    is_first = lane == 0
    is_last = lane == LANES - 1

    def along_z(f):
        up = jnp.where(is_last, 0.0, pltpu.roll(f, LANES - 1, 1))
        down = jnp.where(is_first, 0.0, pltpu.roll(f, 1, 1))
        return up - down

    def along_z_outer(f, outer):
        up = jnp.where(is_last, -outer, pltpu.roll(f, LANES - 1, 1))
        down = jnp.where(is_first, outer, pltpu.roll(f, 1, 1))
        return up - down

    def tile_work(i, p, t, interior):
        r = TOP + pl.multiple_of(t * TILE, 8)
        here = pl.ds(r, TILE)
        u = [w[i, j, p, here, :] for j in range(3)]
        lam = [w[i, 3 + j, p, here, :] for j in range(3)]
        grads, rates = [], []
        for base, values, into in ((0, u, grads), (3, lam, rates)):
            into.append([w[i, base + j, p + 1, here, :] - w[i, base + j, p - 1, here, :] for j in range(3)])
            into.append(
                [w[i, base + j, p, pl.ds(r + 1, TILE), :] - w[i, base + j, p, pl.ds(r - 1, TILE), :] for j in range(3)]
            )
            into.append([along_z(v) for v in values])
        strain = [[grads[k][j] + grads[j][k] for k in range(3)] for j in range(3)]
        rate = [[rates[k][j] + rates[j][k] for k in range(3)] for j in range(3)]
        pairs = ((0, 1), (0, 2), (1, 2))
        square = sum(strain[j][k] * strain[j][k] for j, k in pairs)
        cross = sum(strain[j][k] * rate[j][k] for j, k in pairs)
        square = square + square + sum(strain[j][j] * strain[j][j] for j in range(3))
        cross = cross + cross + sum(strain[j][j] * rate[j][j] for j in range(3))
        mu, dmu = viscosity(square)
        slope = dmu * cross
        half_u = [0.5 * v for v in u]
        half_p = 0.5 * w[i, 6, p, here, :]
        half_q = 0.5 * w[i, 7, p, here, :]

        def flux(j, k):
            t_jk = mu * strain[j][k]
            f_jk = mu * rate[j][k] + slope * strain[j][k] + half_u[k] * lam[j]
            if j == k:
                t_jk, f_jk = t_jk - half_p, f_jk + half_q
            return t_jk, f_jk

        for j in range(3):
            t_jk, f_jk = flux(j, 0)
            tx[i, j, p, pl.ds(r - TOP, TILE), :] = t_jk
            fx[i, j, p, pl.ds(r - TOP, TILE), :] = f_jk
        if not interior:
            return
        q = p - 2
        out_rows = pl.ds(r - TOP, TILE)
        for j in range(3):
            t_jk, f_jk = flux(j, 1)
            ty[j, q, here, :] = t_jk
            fy[j, q, here, :] = f_jk
        outer_t, outer_f = outer_cell(u, lam, 2)
        design = jnp.where(mask_ref[q, out_rows, :] == 1, density_ref[q, out_rows, :], 1.0)
        label = labels_ref[q, out_rows, :]
        ramp = (BRINKMAN_MAX * RAMP_SHAPE) * (1.0 - design) / (RAMP_SHAPE + design)
        penalty = jnp.where(label == 0, ramp, BRINKMAN_MAX)
        target = jnp.where(label == 2, inflow_ref[i], 0.0)
        half_lam = [0.5 * v for v in lam]
        for j in range(3):
            t_jk, f_jk = flux(j, 2)
            shifted = u[j] - target if j == 0 else u[j]
            out_f[i, j, q, out_rows, :] = (
                sum(half_u[k] * grads[k][j] for k in range(3)) - along_z_outer(t_jk, outer_t[j]) + penalty * shifted
            )
            out_a[i, j, q, out_rows, :] = (
                sum(half_lam[k] * grads[j][k] for k in range(3)) - along_z_outer(f_jk, outer_f[j]) + penalty * lam[j]
            )
        out_f[i, 3, q, out_rows, :] = 0.25 * (strain[0][0] + strain[1][1] + strain[2][2])
        out_a[i, 3, q, out_rows, :] = -0.25 * (rate[0][0] + rate[1][1] + rate[2][2])

    def y_edges(i, q):
        p = q + 2
        for first, keep, row, sign in ((TOP, 0, TOP - 1, 1.0), (TOP + ROWS - 8, 7, TOP + ROWS, -1.0)):
            u = [w[i, j, p, first : first + 8, :] for j in range(3)]
            lam = [w[i, 3 + j, p, first : first + 8, :] for j in range(3)]
            outer_t, outer_f = outer_cell(u, lam, 1)
            for j in range(3):
                ty[j, q, row : row + 1, :] = sign * outer_t[j][keep : keep + 1]
                fy[j, q, row : row + 1, :] = sign * outer_f[j][keep : keep + 1]

    def collect(i, p, t, with_x, with_y):
        q = p - 2
        r = pl.multiple_of(t * TILE, 8)
        for out, x_flux, y_flux in ((out_f, tx, ty), (out_a, fx, fy)):
            for j in range(3):
                total = out[i, j, q, pl.ds(r, TILE), :]
                if with_x:
                    total -= x_flux[i, j, p + 1, pl.ds(r, TILE), :] - x_flux[i, j, p - 1, pl.ds(r, TILE), :]
                if with_y:
                    total -= (
                        y_flux[j, q, pl.ds(r + TOP + 1, TILE), :] - y_flux[j, q, pl.ds(r + TOP - 1, TILE), :]
                    )
                out[i, j, q, pl.ds(r, TILE), :] = total

    def over(first, planes, work):
        tiles = ROWS // TILE

        def step(n, _):
            work(first + n // tiles, n % tiles)
            return 0

        lax.fori_loop(0, planes * tiles, step, 0, unroll=UNROLL)

    return tile_work, y_edges, collect, over


def clear_edges(w, i, first, planes):
    zero = jnp.zeros((TOP, LANES), jnp.float32)

    def clear(p, _):
        for c in range(6):
            w[i, c, first + p, 0:TOP, :] = zero
            w[i, c, first + p, TOP + ROWS : PADDED, :] = zero
        return 0

    lax.fori_loop(0, planes, clear, 0)


def early_kernel(
    core_ref, inflow_ref, flow_ref, adj_ref, near_ref, density_hbm, mask_hbm, labels_hbm,
    flow_out, adj_out, tx_out, fx_out,
    out_f, out_a, density_ref, mask_ref, labels_ref, w, tx, fx, ty, fy, sems, cell_sems, out_sems,
):
    insts = out_f.shape[0]
    core = core_ref[0]
    data = pl.ds(TOP, ROWS)
    reads, writes = [], []
    three = pl.ds(1 - core, 3)
    for i in range(insts):
        copies = []
        for source, base, last in ((flow_ref, 0, 6), (adj_ref, 3, 7)):
            copies.append((source.at[i, 0:3], w.at[i, base : base + 3, 2:6, data, :]))
            copies.append((source.at[i, 3], w.at[i, last, 2:6, data, :]))
        for n in range(2):
            for j in range(3):
                copies.append((near_ref.at[i, n, 2 * j : 2 * j + 2], w.at[i, 3 * n + j, pl.ds(6 - 6 * core, 2), data, :]))
            copies.append((near_ref.at[i, n, 6], w.at[i, 6 + n, 6 - 5 * core, data, :]))
        reads.append([pltpu.make_async_copy(a, b, sems.at[i, k]) for k, (a, b) in enumerate(copies)])
        copies = [(a.at[i, :, three], b.at[i, :, three]) for a, b in ((out_f, flow_out), (out_a, adj_out))]
        copies += [(a.at[i, :, 3:5], b.at[i]) for a, b in ((tx, tx_out), (fx, fx_out))]
        writes.append([pltpu.make_async_copy(a, b, out_sems.at[i, k]) for k, (a, b) in enumerate(copies)])
    cells = ((density_hbm, density_ref), (mask_hbm, mask_ref), (labels_hbm, labels_ref))
    reads[0] += [pltpu.make_async_copy(a, b, cell_sems.at[k]) for k, (a, b) in enumerate(cells)]
    for group in reads:
        for h in group:
            h.start()
    for i in range(insts):
        clear_edges(w, i, 0, 8)
    tile_work, y_edges, collect, over = stencil_tools(
        inflow_ref, w, tx, fx, ty, fy, out_f, out_a, density_ref, mask_ref, labels_ref
    )
    for i in range(insts):
        for h in reads[i]:
            h.wait()
        over(6 - 5 * core, 1, lambda p, t: tile_work(i, p, t, False))
        over(3 - core, 3, lambda p, t: tile_work(i, p, t, True))

        def edges(n, _):
            y_edges(i, 1 - core + n)
            return 0

        lax.fori_loop(0, 3, edges, 0)
        over(4 - 2 * core, 2, lambda p, t: collect(i, p, t, True, True))
        over(3 + core, 1, lambda p, t: collect(i, p, t, False, True))
        for h in writes[i]:
            h.start()
    for group in writes:
        for h in group:
            h.wait()


def late_kernel(core_ref, inflow_ref, flow_ref, adj_ref, far_ref, *refs):
    cells_hbm, (_, _, tx_part, fx_part, flow_out, adj_out, sent), refs = refs[:3], refs[3:10], refs[10:]
    out_f, out_a, density_ref, mask_ref, labels_ref, w, tx, fx, ty, fy, sems, part_sems, cell_sems, out_sems = refs
    insts = out_f.shape[0]
    core = core_ref[0]
    at_end = inflow_ref[insts]
    data = pl.ds(TOP, ROWS)
    pair, partial, own = pl.ds(2 * core, 2), pl.ds(1 + core, 1), pl.ds(2 + 2 * core, 2)
    edge, last = 2 + 3 * core, 3 * core
    reads, parts, writes = [], [], []
    for i in range(insts):
        copies = []
        for n, source in enumerate((flow_ref, adj_ref)):
            vel = slice(3 * n, 3 * n + 3)
            copies.append((source.at[i, 0:3, pair], w.at[i, vel, own, data, :]))
            copies.append((source.at[i, 3, pair], w.at[i, 6 + n, own, data, :]))
            copies.append((far_ref.at[i, n], w.at[i, vel, 1 + 5 * core, data, :]))
        reads.append([pltpu.make_async_copy(a, b, sems.at[i, k]) for k, (a, b) in enumerate(copies)])
        copies = [(a.at[i, :, partial], b.at[i, :, partial]) for a, b in ((flow_out, out_f), (adj_out, out_a))]
        copies += [(a.at[i], b.at[i, :, 3:5]) for a, b in ((tx_part, tx), (fx_part, fx))]
        parts.append([pltpu.make_async_copy(a, b, part_sems.at[i, k]) for k, (a, b) in enumerate(copies)])
        copies = [(a.at[i, :, edge], sent.at[i, n]) for n, a in enumerate((tx, fx))]
        copies += [(a.at[i, :, pair], b.at[i, :, pair]) for a, b in ((out_f, flow_out), (out_a, adj_out))]
        writes.append([pltpu.make_async_copy(a, b, out_sems.at[i, k]) for k, (a, b) in enumerate(copies)])
    here = pl.ds(last, 1)
    cells = zip(cells_hbm, (density_ref, mask_ref, labels_ref))
    reads[0] += [pltpu.make_async_copy(a.at[here], b.at[here], cell_sems.at[k]) for k, (a, b) in enumerate(cells)]
    for i in range(insts):
        for h in reads[i] + parts[i]:
            h.start()
    for i in range(insts):
        clear_edges(w, i, 1 + 3 * core, 3)
    tile_work, y_edges, collect, over = stencil_tools(
        inflow_ref, w, tx, fx, ty, fy, out_f, out_a, density_ref, mask_ref, labels_ref
    )
    sign = at_end * (1.0 - 2.0 * core.astype(jnp.float32))

    def beyond(i, t):
        r = pl.multiple_of(t * TILE, 8)
        here = pl.ds(r + TOP, TILE)
        u = [w[i, j, edge, here, :] for j in range(3)]
        lam = [w[i, 3 + j, edge, here, :] for j in range(3)]
        outer_t, outer_f = outer_cell(u, lam, 0)
        for j in range(3):
            tx[i, j, 1 + 5 * core, pl.ds(r, TILE), :] = sign * outer_t[j]
            fx[i, j, 1 + 5 * core, pl.ds(r, TILE), :] = sign * outer_f[j]

    for i in range(insts):
        for h in reads[i]:
            h.wait()
        over(edge, 1, lambda p, t: tile_work(i, p, t, True))
        for h in writes[i][:2]:
            h.start()
        y_edges(i, last)
        over(edge, 1, lambda p, t: beyond(i, t))
        for h in parts[i]:
            h.wait()
        over(edge, 1, lambda p, t: collect(i, p, t, True, True))
        over(3 + core, 1, lambda p, t: collect(i, p, t, True, False))
        for h in writes[i][2:]:
            h.start()
    for group in writes:
        for h in group:
            h.wait()


def load_kernel(f_ref, a_ref, total, sems):
    insts = f_ref.shape[0]
    work = [(i, n) for i in range(insts) for n in range(2)]
    reads = []
    for k, (i, n) in enumerate(work):
        reads.append(pltpu.make_async_copy((f_ref, a_ref)[n].at[i, 0:3], total.at[i, n], sems.at[k]))
        reads[-1].start()
    for read in reads:
        read.wait()


def load_parts(flow_part, adj_part):
    insts = flow_part.shape[0]
    return pl.pallas_call(
        load_kernel,
        out_shape=jax.ShapeDtypeStruct((insts, 2, 3) + flow_part.shape[2:], jnp.float32),
        in_specs=[pl.BlockSpec(memory_space=pltpu.HBM)] * 2,
        out_specs=pl.BlockSpec(memory_space=pltpu.VMEM),
        scratch_shapes=[pltpu.SemaphoreType.DMA((2 * insts,))],
        compiler_params=pltpu.CompilerParams(vmem_limit_bytes=ADD_LIMIT),
        name="load_parts",
    )(flow_part, adj_part)


def flux_kernel(core_ref, part, flux, total):
    core = core_ref[0]
    sign = 1.0 - 2.0 * core.astype(jnp.float32)
    for i in range(part.shape[0]):
        for n in range(2):
            total[i, n] = part[i, n]
            total[i, n, :, 3 * core] = part[i, n, :, 3 * core] + sign * flux[i, n]


def add_flux(core, part, flux):
    whole = pl.BlockSpec(memory_space=pltpu.VMEM)
    return pl.pallas_call(
        flux_kernel,
        out_shape=jax.ShapeDtypeStruct(part.shape, jnp.float32),
        in_specs=[pl.BlockSpec(memory_space=pltpu.SMEM)] + [whole] * 2,
        out_specs=whole,
        compiler_params=pltpu.CompilerParams(vmem_limit_bytes=ADD_LIMIT),
        cost_estimate=pl.CostEstimate(flops=LATE_COST, bytes_accessed=8_000_000, transcendentals=0),
        name="add_flux",
    )(core, part, flux)


def add_kernel(f_ref, a_ref, part, times, out_f, out_a, total, sems):
    insts = out_f.shape[0]
    writes = []
    for i in range(insts):
        for n in range(2):
            for j in range(3):
                for b in range(2 * PLANES):
                    q, rows = block_cells(b)
                    total[i, n, j, q, rows, :] = part[i, n, j, q, rows, :] + times[b, i, 3 * n + j]
                out = (out_f, out_a)[n].at[i, j]
                writes.append(pltpu.make_async_copy(total.at[i, n, j], out, sems.at[len(writes)]))
                writes[-1].start()
    for write in writes:
        write.wait()


def add_time(flow_part, adj_part, part, time_part):
    space = pl.BlockSpec(memory_space=pltpu.HBM)
    insts = flow_part.shape[0]
    shape = jax.ShapeDtypeStruct(flow_part.shape, jnp.float32)
    return pl.pallas_call(
        add_kernel,
        out_shape=(shape, shape),
        in_specs=[space] * 2 + [pl.BlockSpec(memory_space=pltpu.VMEM)] * 2,
        out_specs=[space] * 2,
        scratch_shapes=[pltpu.VMEM(part.shape, jnp.float32), pltpu.SemaphoreType.DMA((6 * insts,))],
        compiler_params=pltpu.CompilerParams(vmem_limit_bytes=ADD_LIMIT),
        input_output_aliases={0: 0, 1: 1},
        name="add_time",
    )(flow_part, adj_part, part, time_part)


def stencil(kernel, name, cost, out_shapes, core, inflow, flow, adj, halos, cells, *parts):
    insts = flow.shape[0]
    space = pl.BlockSpec(memory_space=pltpu.HBM)
    scalar = pl.BlockSpec(memory_space=pltpu.SMEM)
    like = lambda a: pltpu.VMEM(a.shape, a.dtype)
    late = len(parts) > 0
    return pl.pallas_call(
        kernel,
        out_shape=[jax.ShapeDtypeStruct(s, jnp.float32) for s in out_shapes],
        in_specs=[scalar] * 2 + [space] * (2 + len(halos) + len(cells) + len(parts)),
        out_specs=[space] * len(out_shapes),
        scratch_shapes=[like(flow), like(flow)]
        + [like(a) for a in cells]
        + [pltpu.VMEM((insts, 8, 8, PADDED, LANES), jnp.float32)]
        + [pltpu.VMEM((insts, 3, 8, ROWS, LANES), jnp.float32)] * 2
        + [pltpu.VMEM((3, PLANES, PADDED, LANES), jnp.float32)] * 2
        + [pltpu.SemaphoreType.DMA((insts, 12))]
        + ([pltpu.SemaphoreType.DMA((insts, 4))] if late else [])
        + [pltpu.SemaphoreType.DMA((3,)), pltpu.SemaphoreType.DMA((insts, 4))],
        compiler_params=pltpu.CompilerParams(vmem_limit_bytes=VMEM_LIMIT),
        cost_estimate=pl.CostEstimate(flops=cost, bytes_accessed=8_000_000, transcendentals=400_000),
        input_output_aliases={5 + len(halos) + len(cells) - 1 + k: k for k in range(2)} if late else {},
        name=name,
    )(core, inflow, flow, adj, *halos, *cells, *parts)


def spectral_row():
    k = np.arange(1, 8)
    return [float(v) for v in TIME_SCALE * 0.5 * np.where(k % 2 == 0, 1.0, -1.0) / np.tan(np.pi * k / NT)]


def time_kernel(x_ref, sent_hbm, out_hbm, out_ref, sems):
    comps, tiles = x_ref.shape[1], x_ref.shape[2] // 8
    writes = [pltpu.make_async_copy(out_ref.at[:, c], out_hbm.at[:, c], sems.at[c]) for c in range(comps)]
    for c in range(comps):
        coef = [v if c < comps // 2 else -v for v in spectral_row()]

        def step(n, _):
            rows = pl.ds(pl.multiple_of(n * 8, 8), 8)
            x = [x_ref[m, c, rows, :] for m in range(NT)]
            for m in range(NT // 2):
                diff = [x[(m - k) % NT] - x[(m + k) % NT] for k in range(1, 8)]
                out_ref[m, c, rows, :] = sum(coef[k - 1] * diff[k - 1] for k in range(1, 8))
                out_ref[m + 8, c, rows, :] = -sum(coef[k - 1] * diff[7 - k] for k in range(1, 8))
            return 0

        lax.fori_loop(0, tiles, step, 0, unroll=4)
        writes[c].start()
    for h in writes:
        h.wait()


def time_derivative(x, sent):
    return pl.pallas_call(
        time_kernel,
        out_shape=jax.ShapeDtypeStruct(x.shape, jnp.float32),
        in_specs=[pl.BlockSpec(memory_space=pltpu.VMEM), pl.BlockSpec(memory_space=pltpu.HBM)],
        out_specs=pl.BlockSpec(memory_space=pltpu.HBM),
        scratch_shapes=[pltpu.VMEM(x.shape, jnp.float32), pltpu.SemaphoreType.DMA((x.shape[1],))],
        compiler_params=pltpu.CompilerParams(vmem_limit_bytes=8 << 20),
        cost_estimate=pl.CostEstimate(flops=12_000_000, bytes_accessed=3_200_000, transcendentals=0),
        input_output_aliases={1: 0},
        name="time_derivative",
    )(x, sent)


def block_cells(b):
    half = ROWS // 2
    return b // 2, slice(b % 2 * half, (b % 2 + 1) * half)


def halo_copies(state_ref, ref, first, near):
    copies = [(state_ref.at[:, j, pl.ds(first, 2)], ref.at[:, 2 * j : 2 * j + 2]) for j in range(3)]
    return copies + [(state_ref.at[:, 3, pl.ds(near, 1)], ref.at[:, 6:7])]


def block_copies(flow_ref, adj_ref, ref, b):
    q, rows = block_cells(b)
    return [(flow_ref.at[:, 0:3, q, rows], ref.at[b, :, 0:3]), (adj_ref.at[:, 0:3, q, rows], ref.at[b, :, 3:6])]


def through_vmem(groups, sems):
    flat = [c for copies, _ in groups for c in copies] + [write for _, write in groups]
    handles = [pltpu.make_async_copy(a, b, sems.at[i]) for i, (a, b) in enumerate(flat)]
    writes = handles[len(handles) - len(groups) :]
    for h in handles[: len(handles) - len(groups)]:
        h.start()
    done = 0
    for (copies, _), write in zip(groups, writes):
        for h in handles[done : done + len(copies)]:
            h.wait()
        done += len(copies)
        write.start()
    for write in writes:
        write.wait()


def pack_kernel(core_ref, flow_ref, adj_ref, blocks_ref, near_ref, far_ref, blocks, near, far, sems):
    core = core_ref[0]
    states = (flow_ref, adj_ref)
    copies = sum([halo_copies(state, near.at[:, n], 2 - 2 * core, 3 - 3 * core) for n, state in enumerate(states)], [])
    halos = [(copies, (near, near_ref))]
    copies = [(state.at[:, 0:3, 3 * core], far.at[:, n]) for n, state in enumerate(states)]
    halos.append((copies, (far, far_ref)))
    groups = []
    for b in range(2 * PLANES):
        groups.append((block_copies(flow_ref, adj_ref, blocks, b), (blocks.at[b], blocks_ref.at[b])))
    through_vmem(halos + groups, sems)


def pack(core, flow, adj):
    insts = flow.shape[0]
    space = pl.BlockSpec(memory_space=pltpu.HBM)
    halo = (insts, 2, 7, ROWS, LANES)
    blocks = (2 * PLANES, insts, 6, ROWS // 2, LANES)
    shapes = [blocks, halo, (insts, 2, 3, ROWS, LANES)]
    copies = 8 + 1 + 2 + 1 + 6 * PLANES
    return pl.pallas_call(
        pack_kernel,
        out_shape=[jax.ShapeDtypeStruct(s, jnp.float32) for s in shapes],
        in_specs=[pl.BlockSpec(memory_space=pltpu.SMEM)] + [space] * 2,
        out_specs=[space] * len(shapes),
        scratch_shapes=[
            pltpu.VMEM(blocks, jnp.float32),
            pltpu.VMEM(halo, jnp.float32),
            pltpu.VMEM(shapes[2], jnp.float32),
            pltpu.SemaphoreType.DMA((copies,)),
        ],
        compiler_params=pltpu.CompilerParams(vmem_limit_bytes=VMEM_LIMIT),
        name="pack",
    )(core, flow, adj)


def on_device(flow, adj, density, mask, labels):
    insts = flow.shape[0]
    count = lax.axis_size("space")
    instances = lax.axis_index("tm") * insts + jnp.arange(insts, dtype=jnp.int32)
    inflow = 1.0 + 0.5 * jnp.sin(2.0 * jnp.pi * instances.astype(jnp.float32) / NT)

    core = lax.axis_index("space") % 2
    at_end = (lax.axis_index("space") == 0) | (lax.axis_index("space") == count - 1)
    core = core.reshape(1)
    scalars = jnp.append(inflow, at_end.astype(jnp.float32))
    blocks, near, far = pack(core, flow, adj)
    near = lax.ppermute(near, "space", [p for i in range(0, count, 2) for p in ((i, i + 1), (i + 1, i))])
    across = [p for i in range(1, count - 1, 2) for p in ((i, i + 1), (i + 1, i))]
    far = lax.ppermute(far, "space", across)
    if GATED:
        blocks, near = lax.optimization_barrier((blocks, near))
    gathered = lax.all_to_all(blocks, "tm", 0, 0, tiled=True)
    cells = (density, mask, labels)
    edge = (insts, 3, 2, ROWS, LANES)
    parts = stencil(
        early_kernel, "early", EARLY_COST, [flow.shape] * 2 + [edge] * 2, core, scalars, flow, adj, [near], cells
    )
    shapes = [flow.shape] * 2 + [(insts, 2, 3, ROWS, LANES)]
    *parts, flux = stencil(late_kernel, "late", LATE_COST, shapes, core, scalars, flow, adj, [far], cells, *parts)
    flux = lax.ppermute(flux, "space", across)
    gathered, *parts = lax.optimization_barrier((gathered, *parts))
    by_time = (NT,) + blocks.shape[2:]
    derived = time_derivative(gathered.reshape(by_time), blocks.reshape(by_time))
    time_part = lax.all_to_all(derived.reshape(blocks.shape), "tm", 0, 0, tiled=True)
    return add_time(*parts, add_flux(core, load_parts(*parts), flux), time_part)


def solution(mesh):
    split = P("tm", None, "space", None, None)
    cells = P("space", None, None)
    return jax.shard_map(
        on_device,
        mesh=mesh,
        in_specs=(split, split, cells, cells, cells),
        out_specs=(split, split),
        check_vma=False,
    )
```
